128 devices in a mesh: gy: 4 (over y_hi, core), gz: 8 (over y_lo, x), fsdp: 4 (over z).
Axes of the slice: x: 4, y: 4 (y_hi: 2, y_lo: 2; y = y_hi * 2 + y_lo), z: 4, core: 2. Of those that a mesh axis runs over, the one named last changes fastest.
Arguments:
- coarse_field: bfloat16 [4, 48, 16, 64, 128], P('fsdp', None, 'gy', 'gz'), may hold values from -6 to 6
- fine_target: bfloat16 [4, 48, 16, 64, 128], P('fsdp', None, 'gy', 'gz'), may hold values from -6 to 6
- kernel_one: float32 [48, 1296], P(None, 'fsdp'), may hold values from -0.15625 to 0.15625
- kernel_two: float32 [48, 1296], P(None, 'fsdp'), may hold values from -0.15625 to 0.15625
- moment_one: float32 [48, 1296], P(None, 'fsdp'), may hold values from -0.0018 to 0.0018
- moment_two: float32 [48, 1296], P(None, 'fsdp'), may hold values from -0.0018 to 0.0018
- second_one: float32 [48, 1296], P(None, 'fsdp'), may hold values from 1e-09 to 1e-07
- second_two: float32 [48, 1296], P(None, 'fsdp'), may hold values from 1e-09 to 1e-07
Outputs:
- prediction: bfloat16 [4, 48, 16, 64, 128], P('fsdp', None, 'gy', 'gz')
- update_one: float32 [48, 1296], P(None, 'fsdp')
- update_two: float32 [48, 1296], P(None, 'fsdp')
The draws below stay inside these ranges and needn't reach their ends.
All inputs are finite; a program needn't handle non-finite values.
Results may differ from the reference program's by a relative error of at most 0.0049.
Values may be sent and summed in bfloat16 or wider, within the bound.
A program may use at most 128 MiB of HBM per device.

```python
import math
import jax
import jax.numpy as jnp
from jax import lax

C = 48
XLEN = 128
NY = 16
NZ = 64
SAMPLES = 4
TAPS = 1296


def shard_levels(rng, dims, split, smallest, high):
    def one(position, blocks):
        draws = jax.random.uniform(jax.random.fold_in(jax.random.fold_in(rng, 6), position), (blocks,), jnp.float32, smallest / len(split), high / len(split))
        return jnp.repeat(jnp.exp(draws), dims[position] // blocks).reshape((-1,) + (1,) * (len(dims) - position - 1))

    gain = one(*split[0])
    for cut in split[1:]:
        gain = gain * one(*cut)
    return gain


def normal_values(key, extent, width, reach, split=(), kind=jnp.bfloat16):
    loudness = shard_levels(key, extent, split, -0.22, 0.18) if split else 1.0
    entries = jax.random.normal(key, extent, jnp.float32) * width * loudness
    return jnp.minimum(jnp.maximum(entries, -reach), reach).astype(kind)


def setup_inputs(seed: int = 0) -> dict:
    seeds = jax.random.split(jax.random.key(seed), 9)
    return {
        "coarse_field": normal_values(seeds[0], (SAMPLES, C, NY, NZ, XLEN), 1.0, 6.0, ((0, 4), (2, 4), (3, 8))),
        "fine_target": normal_values(seeds[1], (SAMPLES, C, NY, NZ, XLEN), 1.0, 6.0, ((0, 4), (2, 4), (3, 8))),
        "kernel_one": normal_values(seeds[2], (C, TAPS), TAPS ** -0.5, 0.15625, ((1, 4),), jnp.float32),
        "kernel_two": normal_values(seeds[3], (C, TAPS), TAPS ** -0.5, 0.15625, ((1, 4),), jnp.float32),
        "moment_one": normal_values(seeds[4], (C, TAPS), 0.0003, 0.0018, ((1, 4),), jnp.float32),
        "moment_two": normal_values(seeds[5], (C, TAPS), 0.0003, 0.0018, ((1, 4),), jnp.float32),
        "second_one": jnp.clip(jnp.exp(math.log(1.0000000116860974e-07) - 4.6051702 * jax.random.uniform(seeds[6], (C, TAPS), jnp.float32) ** shard_levels(seeds[6], (C, TAPS), ((1, 4),), -0.2, 0.2)), 9.999999717180685e-10, 1.0000000116860974e-07),
        "second_two": jnp.clip(jnp.exp(math.log(1.0000000116860974e-07) - 4.6051702 * jax.random.uniform(seeds[7], (C, TAPS), jnp.float32) ** shard_levels(seeds[7], (C, TAPS), ((1, 4),), -0.2, 0.2)), 9.999999717180685e-10, 1.0000000116860974e-07),
    }


first_bias = 0.9999734386011124
second_bias = 0.09520785288629038

def conv_valid(padded, weight):
    cin = padded.shape[0]
    ny = padded.shape[1] - 2
    nz = padded.shape[2] - 2
    nx = padded.shape[3] - 2
    total = jnp.zeros((weight.shape[0], ny * nz * nx), jnp.float32)
    for dy in range(3):
        for dz in range(3):
            columns = jnp.concatenate([padded[:, dy:dy + ny, dz:dz + nz, dx:dx + nx] for dx in range(3)], 0)
            columns = columns.reshape(3 * cin, ny * nz * nx)
            start = (dy * 9 + dz * 3) * cin
            total = total + jnp.dot(weight[:, start:start + 3 * cin], columns, preferred_element_type=jnp.float32)
    return total.reshape(weight.shape[0], ny, nz, nx)

def weight_grad(padded, errors):
    cin = padded.shape[0]
    ny = padded.shape[1] - 2
    nz = padded.shape[2] - 2
    nx = padded.shape[3] - 2
    flat = errors.reshape(errors.shape[0], ny * nz * nx)
    blocks = []
    for dy in range(3):
        for dz in range(3):
            columns = jnp.concatenate([padded[:, dy:dy + ny, dz:dz + nz, dx:dx + nx] for dx in range(3)], 0)
            columns = columns.reshape(3 * cin, ny * nz * nx)
            blocks.append(lax.dot_general(flat, columns, (((1,), (1,)), ((), ())), preferred_element_type=jnp.float32))
    return jnp.concatenate(blocks, 1)

def back_conv(padded, weight):
    outs = padded.shape[0]
    ny = padded.shape[1] - 2
    nz = padded.shape[2] - 2
    nx = padded.shape[3] - 2
    cin = weight.shape[1] // 27
    shaped = weight.reshape(outs, 27, cin)
    total = jnp.zeros((cin, ny * nz * nx), jnp.float32)
    for dy in range(3):
        for dz in range(3):
            group = dy * 3 + dz
            columns = jnp.concatenate([padded[:, 2 - dy:2 - dy + ny, 2 - dz:2 - dz + nz, 2 - dx:2 - dx + nx] for dx in range(3)], 0)
            columns = columns.reshape(3 * outs, ny * nz * nx)
            matrix = jnp.transpose(shaped[:, group * 3:group * 3 + 3, :], (2, 1, 0)).reshape(cin, 3 * outs)
            total = total + jnp.dot(matrix, columns, preferred_element_type=jnp.float32)
    return total.reshape(cin, ny, nz, nx)

def pad_all(field):
    return jnp.pad(field, ((0, 0), (1, 1), (1, 1), (1, 1)))

def adam_direction(grad, moment, second):
    first_new = 0.9 * moment + 0.1 * grad
    second_new = 0.999 * second + 0.001 * grad * grad
    return first_new / first_bias / (jnp.sqrt(second_new / second_bias) + 1e-08)

def reference(coarse_field, fine_target, kernel_one, kernel_two, moment_one, moment_two, second_one, second_two):
    kb1 = kernel_one.astype(jnp.bfloat16)
    kb2 = kernel_two.astype(jnp.bfloat16)

    def one_sample(carry, pair):
        sample, target = pair
        padded_in = pad_all(sample)
        act_one = conv_valid(padded_in, kb1)
        hidden = jnp.maximum(act_one, 0.0).astype(jnp.bfloat16)
        padded_hidden = pad_all(hidden)
        total = sample.astype(jnp.float32) + conv_valid(padded_hidden, kb2)
        result = total.astype(jnp.bfloat16)
        err_two = (total - target.astype(jnp.float32)).astype(jnp.bfloat16)
        grad_two = weight_grad(padded_hidden, err_two)
        back = back_conv(pad_all(err_two), kb2)
        err_one = jnp.where(act_one > 0, back, 0.0).astype(jnp.bfloat16)
        grad_one = weight_grad(padded_in, err_one)
        return ((carry[0] + grad_one, carry[1] + grad_two), result)
    zeros = jnp.zeros(kernel_one.shape, jnp.float32)
    grads, prediction = lax.scan(one_sample, (zeros, zeros), (coarse_field, fine_target))
    norm = jnp.sqrt(jnp.sum(grads[0] * grads[0]) + jnp.sum(grads[1] * grads[1]))
    factor = jnp.minimum(1.0, 1.0 / (norm + 1e-06))
    update_one = adam_direction(factor * grads[0], moment_one, second_one)
    update_two = adam_direction(factor * grads[1], moment_two, second_two)
    return (prediction, update_one, update_two)
```

```python
import jax
import jax.numpy as jnp
from jax import lax
from jax.experimental import pallas as pl
from jax.experimental.pallas import tpu as pltpu
from jax.sharding import PartitionSpec as P

first_bias = 0.9999734386011124
second_bias = 0.09520785288629038

C = 48
TY, TZ, XL = 4, 8, 128
GY, GZ, NF = 4, 8, 4
PLANE = GY * GZ
TAPS = 27 * C
COLS = TAPS // NF
K9 = 9 * C
C3 = 3 * C
MESH = pl.DeviceIdType.MESH
f32, bf16 = jnp.float32, jnp.bfloat16
DIRS = [(0, -1), (0, 1), (-1, 0), (1, 0), (-1, -1), (-1, 1), (1, -1), (1, 1)]


def edge(step, size, sending):
    if step == 0:
        return pl.ds(1, size)
    if sending:
        return pl.ds(1 if step < 0 else size, 1)
    return pl.ds(size + 1 if step < 0 else 0, 1)


def inside(value, count):
    return jnp.logical_and(value >= 0, value < count)


def roll_right(v, lane):
    return jnp.where(lane > 0, pltpu.roll(v, 1, 1), 0.0)


def roll_left(v, lane):
    return jnp.where(lane < XL - 1, pltpu.roll(v, XL - 1, 1), 0.0)


def rows9(buf, y, za, zb):
    parts = []
    for dy in range(3):
        a = buf[y + dy, pl.ds(za, 3)].reshape(C3, XL)
        b = buf[y + dy, pl.ds(zb, 3)].reshape(C3, XL)
        parts.append(jnp.concatenate([a, b], 1))
    return jnp.concatenate(parts, 0)


def interior(n):
    z = 1 + 2 * (n % 3)
    return 1 + n // 3, z, z + 1


def rim(n):
    plane = n < 8
    y = jnp.where(plane, 3 * (n // 4), n - 7)
    za = jnp.where(plane, 2 * (n % 4), 0)
    zb = jnp.where(plane, za + 1, TZ - 1)
    return y, za, zb


def every(n):
    z = 2 * (n % 4)
    return n // 4, z, z + 1


def kernel(
    x_ref, t_ref, k1_ref, k2_ref, m1_ref, m2_ref, s1_ref, s2_ref,
    pred_ref, u1_ref, u2_ref,
    X, H, E, E1, A1, TG, TS, PS, WG, W1, W2, WB, D, P1, P2, R, Z, TT, Q, A,
    hs, hr, ws, wr, gs, gr, zs, zr, qs, qr,
):
    gy = lax.axis_index("gy")
    gz = lax.axis_index("gz")
    fs = lax.axis_index("fsdp")
    core = gy % 2
    place = gy * GZ + gz
    tile = (gy // 2) * GZ + gz
    lane = lax.broadcasted_iota(jnp.int32, (C, XL), 1)

    def plane_device(index):
        return (index // GZ, index % GZ, fs)

    barrier = pltpu.get_barrier_semaphore()

    def greet(n, carry):
        pl.semaphore_signal(
            barrier, inc=1, device_id=plane_device((place + n) % PLANE), device_id_type=MESH
        )
        return carry

    lax.fori_loop(1, PLANE, greet, 0)
    for n in range(1, NF):
        pl.semaphore_signal(
            barrier, inc=1, device_id=(gy, gz, (fs + n) % NF), device_id_type=MESH
        )

    for k, ref in enumerate((k1_ref, k2_ref)):
        WG[k, fs] = jnp.zeros((C, 384), bf16)
        WG[k, fs, :, 0:COLS] = ref[...].astype(bf16)
    for y in range(TY):
        TS[y] = x_ref[:, y].astype(f32).reshape(C * TZ, XL)
        for z in range(TZ):
            X[y + 1, z + 1] = TS[y, pl.ds(z, C, stride=TZ), :].astype(bf16)

    send_ok = [
        jnp.logical_and(inside(gy + dy, GY), inside(gz + dz, GZ)) for dy, dz in DIRS
    ]
    recv_ok = [
        jnp.logical_and(inside(gy - dy, GY), inside(gz - dz, GZ)) for dy, dz in DIRS
    ]

    for d, (dy, dz) in enumerate(DIRS):
        at = (edge(dy, TY, False), edge(dz, TZ, False))

        @pl.when(jnp.logical_not(recv_ok[d]))
        def _():
            for buf in (X, H, E):
                region = buf.at[at]
                region[...] = jnp.zeros(region.shape, bf16)

    def halo(buf, phase, d):
        dy, dz = DIRS[d]
        return pltpu.make_async_remote_copy(
            src_ref=buf.at[edge(dy, TY, True), edge(dz, TZ, True)],
            dst_ref=buf.at[edge(dy, TY, False), edge(dz, TZ, False)],
            send_sem=hs.at[phase, d],
            recv_sem=hr.at[phase, d],
            device_id=(
                jnp.clip(gy + dy, 0, GY - 1), jnp.clip(gz + dz, 0, GZ - 1), fs
            ),
            device_id_type=MESH,
        )

    def halo_start(buf, phase):
        for d in range(8):
            @pl.when(send_ok[d])
            def _():
                halo(buf, phase, d).start()

    def halo_recv(buf, phase):
        for d in range(8):
            @pl.when(recv_ok[d])
            def _():
                halo(buf, phase, d).wait_recv()

    def halo_sent(buf, phase):
        for d in range(8):
            @pl.when(send_ok[d])
            def _():
                halo(buf, phase, d).wait_send()

    def weight(k, n, owner):
        return pltpu.make_async_remote_copy(
            src_ref=WG.at[k, owner],
            dst_ref=WG.at[k, owner],
            send_sem=ws.at[k, n - 1],
            recv_sem=wr.at[k, n - 1],
            device_id=(gy, gz, (fs + n) % NF),
            device_id_type=MESH,
        )

    pl.semaphore_wait(barrier, PLANE - 1 + NF - 1)

    for n in range(1, NF):
        weight(0, n, fs).start()
    halo_start(X, 0)
    for n in range(1, NF):
        weight(1, n, fs).start()

    for y in range(TY):
        TS[y] = t_ref[:, y].astype(f32).reshape(C * TZ, XL)
        for z in range(TZ):
            TG[y, z] = TS[y, pl.ds(z, C, stride=TZ), :]

    def gathered(k):
        return jnp.concatenate([WG[k, f].astype(f32)[:, :COLS] for f in range(NF)], 1)

    def forward_matrix(full, out):
        for dx in range(3):
            out[dx * C:dx * C + C, :] = jnp.concatenate(
                [full[:, (3 * g + dx) * C:(3 * g + dx + 1) * C] for g in range(9)], 1
            ).astype(bf16)

    for n in range(1, NF):
        weight(0, n, (fs - n + NF) % NF).wait_recv()
    forward_matrix(gathered(0), W1)

    def conv(w, buf, y, za, zb, back):
        out = jnp.dot(w[...], rows9(buf, y, za, zb), preferred_element_type=f32)
        res = []
        for h in range(2):
            q = out[:, h * XL:(h + 1) * XL]
            low, mid, high = q[:C], q[C:2 * C], q[2 * C:]
            if back:
                low, high = high, low
            res.append(mid + roll_right(low, lane) + roll_left(high, lane))
        return res

    def conv1(where):
        def body(n, carry):
            y, za, zb = where(n)
            for z, a1 in zip((za, zb), conv(W1, X, y, za, zb, False)):
                A1[y, z] = a1
                H[y + 1, z + 1] = jnp.maximum(a1, 0.0).astype(bf16)
            return carry
        return body

    halo_recv(X, 0)
    lax.fori_loop(0, 10, conv1(rim), 0, unroll=2)
    halo_start(H, 1)
    lax.fori_loop(0, 6, conv1(interior), 0, unroll=2)

    for n in range(1, NF):
        weight(1, n, (fs - n + NF) % NF).wait_recv()
    full2 = gathered(1)
    forward_matrix(full2, W2)

    def conv2(where):
        def body(n, carry):
            y, za, zb = where(n)
            for z, a2 in zip((za, zb), conv(W2, H, y, za, zb, False)):
                total = X[y + 1, z + 1].astype(f32) + a2
                PS[y, pl.ds(z, C, stride=TZ), :] = total
                E[y + 1, z + 1] = (total - TG[y, z]).astype(bf16)
            return carry
        return body

    lax.fori_loop(0, 6, conv2(interior), 0, unroll=2)
    halo_recv(H, 1)
    lax.fori_loop(0, 10, conv2(rim), 0, unroll=2)
    halo_start(E, 2)

    def shifted(e):
        v = e.astype(f32)
        return jnp.concatenate(
            [roll_left(v, lane).astype(bf16), e, roll_right(v, lane).astype(bf16)], 0
        )

    def weight_grad(buf, err):
        D[...] = jnp.zeros((C3, K9), f32)

        def body(n, carry):
            y, za, zb = every(n)
            left = jnp.concatenate([shifted(err(y, za)), shifted(err(y, zb))], 1)
            D[...] += lax.dot_general(
                left, rows9(buf, y, za, zb), (((1,), (1,)), ((), ())),
                preferred_element_type=f32,
            )
            return carry

        lax.fori_loop(0, 16, body, 0, unroll=2)

    def pack(out):
        grad = D[...]
        for f in range(NF):
            pieces = []
            for third in range(3):
                col = COLS * f
                while col < COLS * (f + 1):
                    block, i = col // C, col % C
                    width = min(C - i, COLS * (f + 1) - col)
                    g, dx = block // 3, block % 3
                    pieces.append(
                        grad[dx * C + 16 * third:dx * C + 16 * third + 16,
                             g * C + i:g * C + i + width]
                    )
                    col += width
            pieces.append(jnp.zeros((16, 1024 - 3 * COLS), f32))
            flat = jnp.concatenate(pieces, 1)
            for t in range(16):
                out[t, f] = flat[(t // 8) * 8:(t // 8) * 8 + 8, (t % 8) * 128:(t % 8 + 1) * 128]

    def scatter(k, src):
        def send(n, carry):
            to = (tile + n) % 16
            owner = (2 * (to // GZ) + k) * GZ + to % GZ
            pltpu.make_async_remote_copy(
                src_ref=src.at[to],
                dst_ref=R.at[(place - owner + PLANE) % PLANE],
                send_sem=gs.at[k],
                recv_sem=gr,
                device_id=plane_device(owner),
                device_id_type=MESH,
            ).start()
            return carry

        @pl.when(core == k)
        def _():
            R[0] = src[tile]

        @pl.when(core != k)
        def _():
            send(0, 0)

        lax.fori_loop(1, 16, send, 0)

    def scattered(k, src):
        def wait(count):
            pltpu.make_async_remote_copy(
                src_ref=src.at[pl.ds(0, count)], dst_ref=R.at[pl.ds(0, count)],
                send_sem=gs.at[k], recv_sem=gr, device_id=plane_device(place),
                device_id_type=MESH,
            ).wait_send()

        @pl.when(core == k)
        def _():
            wait(15)

        @pl.when(core != k)
        def _():
            wait(16)

    weight_grad(H, lambda y, z: E[y + 1, z + 1])
    pack(P2)
    scatter(1, P2)

    turned = full2.T
    for dx in range(3):
        WB[dx * C:dx * C + C, :] = jnp.concatenate(
            [
                turned[(26 - 3 * g - 2 + dx) * C:(26 - 3 * g - 2 + dx + 1) * C, :]
                for g in range(9)
            ],
            1,
        ).astype(bf16)

    halo_recv(E, 2)

    def back(n, carry):
        y, za, zb = every(n)
        for z, b in zip((za, zb), conv(WB, E, y, za, zb, True)):
            E1[y, z] = jnp.where(A1[y, z] > 0, b, 0.0).astype(bf16)
        return carry

    lax.fori_loop(0, 16, back, 0, unroll=2)
    weight_grad(X, lambda y, z: E1[y, z])
    pack(P1)
    scatter(0, P1)

    for y in range(TY):
        pred_ref[:, y] = PS[y].reshape(C, TZ, XL).astype(bf16)

    pltpu.make_async_remote_copy(
        src_ref=R.at[pl.ds(1, PLANE - 1)], dst_ref=R.at[pl.ds(1, PLANE - 1)],
        send_sem=gs.at[0], recv_sem=gr, device_id=plane_device(place), device_id_type=MESH,
    ).wait_recv()
    own = R[0]
    for n in range(1, PLANE):
        own = own + R[n]
    Z[fs] = own
    for n in range(1, NF):
        pltpu.make_async_remote_copy(
            src_ref=Z.at[fs], dst_ref=Z.at[fs], send_sem=zs.at[n - 1], recv_sem=zr.at[n - 1],
            device_id=(gy, gz, (fs + n) % NF), device_id_type=MESH,
        ).start()
    for n in range(1, NF):
        other = (fs - n + NF) % NF
        pltpu.make_async_remote_copy(
            src_ref=Z.at[other], dst_ref=Z.at[other], send_sem=zs.at[n - 1],
            recv_sem=zr.at[n - 1], device_id=(gy, gz, other), device_id_type=MESH,
        ).wait_recv()
    total = Z[0] + Z[1] + Z[2] + Z[3]
    TT[...] = total
    Q[0] = TT[fs]
    Q[1] = jnp.sum(total * total, 0)

    slot = core * 16 + tile
    A[slot] = Q[...]

    def spread(n, carry):
        pltpu.make_async_remote_copy(
            src_ref=Q, dst_ref=A.at[slot], send_sem=qs, recv_sem=qr,
            device_id=plane_device((place + n) % PLANE), device_id_type=MESH,
        ).start()
        return carry

    lax.fori_loop(1, PLANE, spread, 0)
    gather = pltpu.make_async_remote_copy(
        src_ref=A.at[pl.ds(0, PLANE - 1)], dst_ref=A.at[pl.ds(0, PLANE - 1)],
        send_sem=qs, recv_sem=qr, device_id=plane_device(place), device_id_type=MESH,
    )
    gather.wait_recv()

    squares = A[0, 1]
    for n in range(1, PLANE):
        squares = squares + A[n, 1]
    norm = jnp.sqrt(jnp.sum(squares, keepdims=True))
    factor = jnp.minimum(1.0, 1.0 / (norm + 1e-06))
    for k, (m_ref, s_ref, u_ref) in enumerate(
        ((m1_ref, s1_ref, u1_ref), (m2_ref, s2_ref, u2_ref))
    ):
        flat = jnp.concatenate(
            [
                jnp.concatenate([A[k * 16 + r * 8 + t, 0] for t in range(8)], 1)
                for r in range(2)
            ],
            0,
        )
        for third in range(3):
            at = pl.ds(16 * third, 16)
            grad = factor * flat[:, COLS * third:COLS * (third + 1)]
            first = 0.9 * m_ref[at, :] + 0.1 * grad
            second = 0.999 * s_ref[at, :] + 0.001 * grad * grad
            u_ref[at, :] = first / first_bias / (jnp.sqrt(second / second_bias) + 1e-08)

    for n in range(1, NF):
        weight(0, n, fs).wait_send()
        weight(1, n, fs).wait_send()
        pltpu.make_async_remote_copy(
            src_ref=Z.at[fs], dst_ref=Z.at[fs], send_sem=zs.at[n - 1], recv_sem=zr.at[n - 1],
            device_id=(gy, gz, (fs + n) % NF), device_id_type=MESH,
        ).wait_send()
    for phase, buf in enumerate((X, H, E)):
        halo_sent(buf, phase)
    scattered(0, P1)
    scattered(1, P2)
    gather.wait_send()


def shards(
    coarse_field, fine_target, kernel_one, kernel_two,
    moment_one, moment_two, second_one, second_two,
):
    vmem = pl.BlockSpec(memory_space=pltpu.VMEM)
    dma = pltpu.SemaphoreType.DMA
    padded = pltpu.VMEM((TY + 2, TZ + 2, C, XL), bf16)
    prediction, update_one, update_two = pl.pallas_call(
        kernel,
        out_shape=[
            jax.ShapeDtypeStruct((C, TY, TZ, XL), bf16),
            jax.ShapeDtypeStruct((C, COLS), f32),
            jax.ShapeDtypeStruct((C, COLS), f32),
        ],
        in_specs=[vmem] * 8,
        out_specs=[vmem] * 3,
        scratch_shapes=[
            padded, padded, padded,
            pltpu.VMEM((TY, TZ, C, XL), bf16),
            pltpu.VMEM((TY, TZ, C, XL), f32),
            pltpu.VMEM((TY, TZ, C, XL), f32),
            pltpu.VMEM((TY, C * TZ, XL), f32),
            pltpu.VMEM((TY, C * TZ, XL), f32),
            pltpu.VMEM((2, NF, C, 384), bf16),
            pltpu.VMEM((C3, K9), bf16),
            pltpu.VMEM((C3, K9), bf16),
            pltpu.VMEM((C3, K9), bf16),
            pltpu.VMEM((C3, K9), f32),
            pltpu.VMEM((16, NF, 8, 128), f32),
            pltpu.VMEM((16, NF, 8, 128), f32),
            pltpu.VMEM((PLANE, NF, 8, 128), f32),
            pltpu.VMEM((NF, NF, 8, 128), f32),
            pltpu.VMEM((NF, 8, 128), f32),
            pltpu.VMEM((2, 8, 128), f32),
            pltpu.VMEM((PLANE, 2, 8, 128), f32),
            dma((3, 8)), dma((3, 8)),
            dma((2, 3)), dma((2, 3)),
            dma((2,)), dma,
            dma((3,)), dma((3,)),
            dma, dma,
        ],
        compiler_params=pltpu.CompilerParams(
            collective_id=0, has_side_effects=True, vmem_limit_bytes=40 << 20
        ),
    )(
        coarse_field[0], fine_target[0], kernel_one, kernel_two,
        moment_one, moment_two, second_one, second_two,
    )
    return prediction[None], update_one, update_two


def solution(mesh):
    field = P("fsdp", None, "gy", "gz", None)
    state = P(None, "fsdp")
    return jax.shard_map(
        shards,
        mesh=mesh,
        in_specs=(field, field) + (state,) * 6,
        out_specs=(field, state, state),
        check_vma=False,
    )
```

```python
import jax
import jax.numpy as jnp
from jax import lax
from jax.experimental import pallas as pl
from jax.experimental.pallas import tpu as pltpu
from jax.sharding import PartitionSpec as P

first_bias = 0.9999734386011124
second_bias = 0.09520785288629038

C = 48
TY, TZ, XL = 4, 8, 128
GY, GZ, NF = 4, 8, 4
PLANE = GY * GZ
TAPS = 27 * C
COLS = TAPS // NF
K9 = 9 * C
C3 = 3 * C
MESH = pl.DeviceIdType.MESH
f32, bf16 = jnp.float32, jnp.bfloat16
DIRS = [(0, -1), (0, 1), (-1, 0), (1, 0), (-1, -1), (-1, 1), (1, -1), (1, 1)]


def edge(step, size, sending):
    if step == 0:
        return pl.ds(1, size)
    if sending:
        return pl.ds(1 if step < 0 else size, 1)
    return pl.ds(size + 1 if step < 0 else 0, 1)


def inside(value, count):
    return jnp.logical_and(value >= 0, value < count)


def roll_right(v, lane):
    return jnp.where(lane > 0, pltpu.roll(v, 1, 1), 0.0)


def roll_left(v, lane):
    return jnp.where(lane < XL - 1, pltpu.roll(v, XL - 1, 1), 0.0)


def rows9(buf, cells):
    return jnp.concatenate(
        [
            jnp.concatenate(
                [buf[y + dy, z:z + 3].reshape(C3, XL) for y, z in cells], 1
            )
            for dy in range(3)
        ],
        0,
    )


INNER = [((y, z), (y, z + 1)) for y in (1, 2) for z in (1, 3, 5)]
RIM = [((y, z), (y, z + 1)) for y in (0, 3) for z in (0, 2, 4, 6)]
RIM += [((y, 0), (y, TZ - 1)) for y in (1, 2)]
PLANES = [tuple((y, z) for z in range(TZ)) for y in range(TY)]


def kernel(
    x_hbm, t_hbm, k1_hbm, k2_hbm, m1_hbm, m2_hbm, s1_hbm, s2_hbm,
    pred_hbm, u1_hbm, u2_hbm,
    x_ref, t_ref, k1_ref, k2_ref, m1_ref, m2_ref, s1_ref, s2_ref,
    pred_ref, u1_ref, u2_ref, ls, os, X, H, E, E1, A1, TG, TS, PS, WG, W1, W2, WB, P1, P2, R, Z, TT, Q, A,
    hs, hr, ws, wr, gs, gr, zs, zr, qs, qr,
):
    gy = lax.axis_index("gy")
    gz = lax.axis_index("gz")
    fs = lax.axis_index("fsdp")
    core = gy % 2
    place = gy * GZ + gz
    tile = (gy // 2) * GZ + gz
    lane = lax.broadcasted_iota(jnp.int32, (C, XL), 1)

    loads = [
        pltpu.make_async_copy(source, ref, ls.at[n])
        for n, (source, ref) in enumerate((
            (k1_hbm, k1_ref), (x_hbm, x_ref), (k2_hbm, k2_ref), (t_hbm, t_ref),
            (m1_hbm, m1_ref), (s1_hbm, s1_ref), (m2_hbm, m2_ref), (s2_hbm, s2_ref),
        ))
    ]
    owed = {}

    def settle(name):
        owed.pop(name)()

    def finish():
        for name in list(owed):
            settle(name)

    for n, load in enumerate(loads):
        load.start()
        owed["load", n] = load.wait
    stores = [
        pltpu.make_async_copy(ref, result, os.at[n])
        for n, (ref, result) in enumerate((
            (pred_ref, pred_hbm), (u1_ref, u1_hbm), (u2_ref, u2_hbm)
        ))
    ]

    def plane_device(index):
        return (index // GZ, index % GZ, fs)

    barrier = pltpu.get_barrier_semaphore()

    def greet(n, carry):
        pl.semaphore_signal(
            barrier, inc=1, device_id=plane_device((place + n) % PLANE), device_id_type=MESH
        )
        return carry

    lax.fori_loop(1, PLANE, greet, 0)
    for n in range(1, NF):
        pl.semaphore_signal(
            barrier, inc=1, device_id=(gy, gz, (fs + n) % NF), device_id_type=MESH
        )

    for k, ref in enumerate((k1_ref, k2_ref)):
        settle(("load", 2 * k))
        WG[k, fs] = jnp.zeros((C, 384), bf16)
        WG[k, fs, :, 0:COLS] = ref[...].astype(bf16)
    settle(("load", 1))
    for y in range(TY):
        TS[y] = x_ref[:, y].astype(f32).reshape(C * TZ, XL)
        for z in range(TZ):
            X[y + 1, z + 1] = TS[y, pl.ds(z, C, stride=TZ), :].astype(bf16)

    send_ok = [
        jnp.logical_and(inside(gy + dy, GY), inside(gz + dz, GZ)) for dy, dz in DIRS
    ]
    recv_ok = [
        jnp.logical_and(inside(gy - dy, GY), inside(gz - dz, GZ)) for dy, dz in DIRS
    ]

    for d, (dy, dz) in enumerate(DIRS):
        at = (edge(dy, TY, False), edge(dz, TZ, False))

        @pl.when(jnp.logical_not(recv_ok[d]))
        def _():
            for buf in (X, H, E):
                region = buf.at[at]
                region[...] = jnp.zeros(region.shape, bf16)

    def halo(buf, phase, d):
        dy, dz = DIRS[d]
        return pltpu.make_async_remote_copy(
            src_ref=buf.at[edge(dy, TY, True), edge(dz, TZ, True)],
            dst_ref=buf.at[edge(dy, TY, False), edge(dz, TZ, False)],
            send_sem=hs.at[phase, d],
            recv_sem=hr.at[phase, d],
            device_id=(
                jnp.clip(gy + dy, 0, GY - 1), jnp.clip(gz + dz, 0, GZ - 1), fs
            ),
            device_id_type=MESH,
        )

    def halo_start(buf, phase):
        def arrived():
            for d in range(8):
                @pl.when(recv_ok[d])
                def _():
                    halo(buf, phase, d).wait_recv()

        def sent():
            for d in range(8):
                @pl.when(send_ok[d])
                def _():
                    halo(buf, phase, d).wait_send()

        for d in range(8):
            @pl.when(send_ok[d])
            def _():
                halo(buf, phase, d).start()
        owed["halo", phase], owed["halo sent", phase] = arrived, sent

    def weight(k, n, owner):
        return pltpu.make_async_remote_copy(
            src_ref=WG.at[k, owner],
            dst_ref=WG.at[k, owner],
            send_sem=ws.at[k, n - 1],
            recv_sem=wr.at[k, n - 1],
            device_id=(gy, gz, (fs + n) % NF),
            device_id_type=MESH,
        )

    def weight_start(k):
        def arrived():
            for n in range(1, NF):
                weight(k, n, (fs - n + NF) % NF).wait_recv()

        def sent():
            for n in range(1, NF):
                weight(k, n, fs).wait_send()

        for n in range(1, NF):
            weight(k, n, fs).start()
        owed["weight", k], owed["weight sent", k] = arrived, sent

    pl.semaphore_wait(barrier, PLANE - 1 + NF - 1)

    weight_start(0)
    halo_start(X, 0)
    weight_start(1)

    settle(("load", 3))
    for y in range(TY):
        TS[y] = t_ref[:, y].astype(f32).reshape(C * TZ, XL)
        for z in range(TZ):
            TG[y, z] = TS[y, pl.ds(z, C, stride=TZ), :]

    def gathered(k):
        return jnp.concatenate([WG[k, f].astype(f32)[:, :COLS] for f in range(NF)], 1)

    def forward_matrix(full, out):
        for dx in range(3):
            out[dx * C:dx * C + C, :] = jnp.concatenate(
                [full[:, (3 * g + dx) * C:(3 * g + dx + 1) * C] for g in range(9)], 1
            ).astype(bf16)

    settle(("weight", 0))
    forward_matrix(gathered(0), W1)

    def conv(w, buf, cells, back=False):
        out = jnp.dot(w[...], rows9(buf, cells), preferred_element_type=f32)
        res = []
        for h in range(len(cells)):
            q = out[:, h * XL:(h + 1) * XL]
            low, mid, high = q[:C], q[C:2 * C], q[2 * C:]
            if back:
                low, high = high, low
            res.append(mid + roll_right(low, lane) + roll_left(high, lane))
        return zip(cells, res)

    def conv1(groups):
        for cells in groups:
            for (y, z), a1 in conv(W1, X, cells):
                A1[y, z] = a1
                H[y + 1, z + 1] = jnp.maximum(a1, 0.0).astype(bf16)

    settle(("halo", 0))
    conv1(RIM)
    halo_start(H, 1)
    conv1(INNER)

    settle(("weight", 1))
    full2 = gathered(1)
    forward_matrix(full2, W2)

    def conv2(groups):
        for cells in groups:
            for (y, z), a2 in conv(W2, H, cells):
                total = X[y + 1, z + 1].astype(f32) + a2
                PS[y, pl.ds(z, C, stride=TZ), :] = total
                E[y + 1, z + 1] = (total - TG[y, z]).astype(bf16)

    conv2(INNER)
    settle(("halo", 1))
    conv2(RIM)
    halo_start(E, 2)

    def shifted(e):
        v = e.astype(f32)
        return jnp.concatenate(
            [roll_left(v, lane).astype(bf16), e, roll_right(v, lane).astype(bf16)], 0
        )

    def weight_grad(buf, err):
        grad = jnp.zeros((K9, C3), f32)
        for cells in PLANES:
            right = jnp.concatenate([shifted(err(y, z)) for y, z in cells], 1)
            grad += lax.dot_general(
                rows9(buf, cells), right, (((1,), (1,)), ((), ())),
                preferred_element_type=f32,
            )
        return grad.T

    def pack(grad, out):
        for f in range(NF):
            pieces = []
            for third in range(3):
                col = COLS * f
                while col < COLS * (f + 1):
                    block, i = col // C, col % C
                    width = min(C - i, COLS * (f + 1) - col)
                    g, dx = block // 3, block % 3
                    pieces.append(
                        grad[dx * C + 16 * third:dx * C + 16 * third + 16,
                             g * C + i:g * C + i + width]
                    )
                    col += width
            pieces.append(jnp.zeros((16, 1024 - 3 * COLS), f32))
            flat = jnp.concatenate(pieces, 1)
            for t in range(16):
                out[t, f] = flat[(t // 8) * 8:(t // 8) * 8 + 8, (t % 8) * 128:(t % 8 + 1) * 128]

    def scatter(k, src):
        def send(n, carry):
            to = (tile + n) % 16
            owner = (2 * (to // GZ) + k) * GZ + to % GZ
            pltpu.make_async_remote_copy(
                src_ref=src.at[to],
                dst_ref=R.at[(place - owner + PLANE) % PLANE],
                send_sem=gs.at[k],
                recv_sem=gr,
                device_id=plane_device(owner),
                device_id_type=MESH,
            ).start()
            return carry

        @pl.when(core == k)
        def _():
            R[0] = src[tile]

        @pl.when(core != k)
        def _():
            send(0, 0)

        lax.fori_loop(1, 16, send, 0)

        def sent():
            for count, mine in ((15, core == k), (16, core != k)):
                @pl.when(mine)
                def _():
                    pltpu.make_async_remote_copy(
                        src_ref=src.at[pl.ds(0, count)], dst_ref=R.at[pl.ds(0, count)],
                        send_sem=gs.at[k], recv_sem=gr, device_id=plane_device(place),
                        device_id_type=MESH,
                    ).wait_send()

        def parts():
            @pl.when(core == k)
            def _():
                pltpu.make_async_remote_copy(
                    src_ref=R.at[pl.ds(1, PLANE - 1)], dst_ref=R.at[pl.ds(1, PLANE - 1)],
                    send_sem=gs.at[k], recv_sem=gr, device_id=plane_device(place),
                    device_id_type=MESH,
                ).wait_recv()

        owed["parts", k], owed["scatter sent", k] = parts, sent

    grad2 = weight_grad(H, lambda y, z: E[y + 1, z + 1])
    pack(grad2, P2)
    scatter(1, P2)

    turned = full2.T
    for dx in range(3):
        WB[dx * C:dx * C + C, :] = jnp.concatenate(
            [
                turned[(26 - 3 * g - 2 + dx) * C:(26 - 3 * g - 2 + dx + 1) * C, :]
                for g in range(9)
            ],
            1,
        ).astype(bf16)

    def back(groups):
        for cells in groups:
            for (y, z), b in conv(WB, E, cells, True):
                E1[y, z] = jnp.where(A1[y, z] > 0, b, 0.0).astype(bf16)

    back(INNER)
    settle(("halo", 2))
    back(RIM)
    grad1 = weight_grad(X, lambda y, z: E1[y, z])
    pack(grad1, P1)
    scatter(0, P1)

    for y in range(TY):
        pred_ref[:, y] = PS[y].reshape(C, TZ, XL).astype(bf16)
    stores[0].start()
    owed["store", 0] = stores[0].wait

    settle(("parts", 1))
    settle(("parts", 0))
    own = R[0]
    for n in range(1, PLANE):
        own = own + R[n]
    Z[fs] = own

    def along(n, owner):
        return pltpu.make_async_remote_copy(
            src_ref=Z.at[owner], dst_ref=Z.at[owner], send_sem=zs.at[n - 1],
            recv_sem=zr.at[n - 1], device_id=(gy, gz, (fs + n) % NF), device_id_type=MESH,
        )

    def sums():
        for n in range(1, NF):
            along(n, (fs - n + NF) % NF).wait_recv()

    def sums_sent():
        for n in range(1, NF):
            along(n, fs).wait_send()

    for n in range(1, NF):
        along(n, fs).start()
    owed["sums"], owed["sums sent"] = sums, sums_sent
    settle("sums")
    total = Z[0] + Z[1] + Z[2] + Z[3]
    TT[...] = total
    Q[0] = TT[fs]
    Q[1] = jnp.sum(total * total, 0)

    slot = core * 16 + tile
    A[slot] = Q[...]

    def spread(n, carry):
        pltpu.make_async_remote_copy(
            src_ref=Q, dst_ref=A.at[slot], send_sem=qs, recv_sem=qr,
            device_id=plane_device((place + n) % PLANE), device_id_type=MESH,
        ).start()
        return carry

    lax.fori_loop(1, PLANE, spread, 0)
    gather = pltpu.make_async_remote_copy(
        src_ref=A.at[pl.ds(0, PLANE - 1)], dst_ref=A.at[pl.ds(0, PLANE - 1)],
        send_sem=qs, recv_sem=qr, device_id=plane_device(place), device_id_type=MESH,
    )
    owed["gather"], owed["gather sent"] = gather.wait_recv, gather.wait_send
    settle("gather")

    squares = A[0, 1]
    for n in range(1, PLANE):
        squares = squares + A[n, 1]
    norm = jnp.sqrt(jnp.sum(squares, keepdims=True))
    factor = jnp.minimum(1.0, 1.0 / (norm + 1e-06))
    for n in range(4, 8):
        settle(("load", n))
    for k, (m_ref, s_ref, u_ref) in enumerate(
        ((m1_ref, s1_ref, u1_ref), (m2_ref, s2_ref, u2_ref))
    ):
        flat = jnp.concatenate(
            [
                jnp.concatenate([A[k * 16 + r * 8 + t, 0] for t in range(8)], 1)
                for r in range(2)
            ],
            0,
        )
        for third in range(3):
            at = pl.ds(16 * third, 16)
            grad = factor * flat[:, COLS * third:COLS * (third + 1)]
            first = 0.9 * m_ref[at, :] + 0.1 * grad
            second = 0.999 * s_ref[at, :] + 0.001 * grad * grad
            u_ref[at, :] = first / first_bias / (jnp.sqrt(second / second_bias) + 1e-08)
        stores[1 + k].start()
        owed["store", 1 + k] = stores[1 + k].wait

    finish()


def hand_on(*refs):
    sources, results, held, sems = refs[:3], refs[3:6], refs[6:9], refs[9]
    inward = [
        pltpu.make_async_copy(sources[n], held[n], sems.at[0, n]) for n in range(3)
    ]
    outward = [
        pltpu.make_async_copy(held[n], results[n], sems.at[1, n]) for n in range(3)
    ]
    for copy in inward:
        copy.start()
    for n in range(3):
        inward[n].wait()
        outward[n].start()
    for copy in outward:
        copy.wait()


def shards(
    coarse_field, fine_target, kernel_one, kernel_two,
    moment_one, moment_two, second_one, second_two,
):
    hbm = pl.BlockSpec(memory_space=pltpu.HBM)
    dma = pltpu.SemaphoreType.DMA
    padded = pltpu.VMEM((TY + 2, TZ + 2, C, XL), bf16)
    results = [
        jax.ShapeDtypeStruct((C, TY, TZ, XL), bf16),
        jax.ShapeDtypeStruct((C, COLS), f32),
        jax.ShapeDtypeStruct((C, COLS), f32),
    ]
    computed = pl.pallas_call(
        kernel,
        out_shape=results,
        in_specs=[hbm] * 8,
        out_specs=[hbm] * 3,
        scratch_shapes=[
            pltpu.VMEM((C, TY, TZ, XL), bf16), pltpu.VMEM((C, TY, TZ, XL), bf16),
        ] + [pltpu.VMEM((C, COLS), f32)] * 6 + [
            pltpu.VMEM((C, TY, TZ, XL), bf16),
            pltpu.VMEM((C, COLS), f32), pltpu.VMEM((C, COLS), f32),
            dma((8,)), dma((3,)),
            padded, padded, padded,
            pltpu.VMEM((TY, TZ, C, XL), bf16),
            pltpu.VMEM((TY, TZ, C, XL), f32),
            pltpu.VMEM((TY, TZ, C, XL), f32),
            pltpu.VMEM((TY, C * TZ, XL), f32),
            pltpu.VMEM((TY, C * TZ, XL), f32),
            pltpu.VMEM((2, NF, C, 384), bf16),
            pltpu.VMEM((C3, K9), bf16),
            pltpu.VMEM((C3, K9), bf16),
            pltpu.VMEM((C3, K9), bf16),
            pltpu.VMEM((16, NF, 8, 128), f32),
            pltpu.VMEM((16, NF, 8, 128), f32),
            pltpu.VMEM((PLANE, NF, 8, 128), f32),
            pltpu.VMEM((NF, NF, 8, 128), f32),
            pltpu.VMEM((NF, 8, 128), f32),
            pltpu.VMEM((2, 8, 128), f32),
            pltpu.VMEM((PLANE, 2, 8, 128), f32),
            dma((3, 8)), dma((3, 8)),
            dma((2, 3)), dma((2, 3)),
            dma((2,)), dma,
            dma((3,)), dma((3,)),
            dma, dma,
        ],
        compiler_params=pltpu.CompilerParams(
            collective_id=0, has_side_effects=True, vmem_limit_bytes=60 << 20
        ),
    )(
        coarse_field[0], fine_target[0], kernel_one, kernel_two,
        moment_one, moment_two, second_one, second_two,
    )
    prediction, update_one, update_two = pl.pallas_call(
        hand_on,
        out_shape=results,
        in_specs=[hbm] * 3,
        out_specs=[hbm] * 3,
        scratch_shapes=[pltpu.VMEM(r.shape, r.dtype) for r in results] + [dma((2, 3))],
        compiler_params=pltpu.CompilerParams(vmem_limit_bytes=60 << 20),
    )(*computed)
    return prediction[None], update_one, update_two


def solution(mesh):
    field = P("fsdp", None, "gy", "gz", None)
    state = P(None, "fsdp")
    return jax.shard_map(
        shards,
        mesh=mesh,
        in_specs=(field, field) + (state,) * 6,
        out_specs=(field, state, state),
        check_vma=False,
    )
```

```python
import jax
import jax.numpy as jnp
from jax import lax
from jax.experimental import pallas as pl
from jax.experimental.pallas import tpu as pltpu
from jax.sharding import PartitionSpec as P

first_bias = 0.9999734386011124
second_bias = 0.09520785288629038

C = 48
TY, TZ, XL = 4, 8, 128
GY, GZ, NF = 4, 8, 4
PLANE = GY * GZ
TAPS = 27 * C
COLS = TAPS // NF
K9 = 9 * C
C3 = 3 * C
MESH = pl.DeviceIdType.MESH
f32, bf16 = jnp.float32, jnp.bfloat16
DIRS = [(-1, -1), (-1, 1), (-1, 0), (1, -1), (1, 1), (1, 0), (0, -1), (0, 1)]


def edge(step, size, width, sending):
    if step == 0:
        return pl.ds(width, size)
    if sending:
        return pl.ds(width if step < 0 else size, width)
    return pl.ds(size + width if step < 0 else 0, width)


def inside(value, count):
    return jnp.logical_and(value >= 0, value < count)


def roll_right(v, lane):
    return jnp.where(lane > 0, pltpu.roll(v, 1, 1), 0.0)


def roll_left(v, lane):
    return jnp.where(lane < XL - 1, pltpu.roll(v, XL - 1, 1), 0.0)


def rows9(buf, width, cells):
    off = width - 1
    return jnp.concatenate(
        [
            jnp.concatenate(
                [buf[y + dy + off, z + off:z + off + 3].reshape(C3, XL) for y, z in cells], 1
            )
            for dy in range(3)
        ],
        0,
    )


LOW = [((0, z), (0, z + 1)) for z in range(0, TZ, 2)]
HIGH = [((TY - 1, z), (TY - 1, z + 1)) for z in range(0, TZ, 2)]
SIDES = [((y, 0), (y, TZ - 1)) for y in range(1, TY - 1)]
INNER = [((y, z), (y, z + 1)) for y in range(1, TY - 1) for z in range(1, TZ - 1, 2)]
WIDE = [((y, z), (y, z + 1)) for y in range(-1, TY + 1) for z in range(-1, TZ + 1, 2)]
PLANES = [tuple((y, z) for z in range(TZ)) for y in range(TY)]


def kernel(
    x_hbm, t_hbm, k1_hbm, k2_hbm, m1_hbm, m2_hbm, s1_hbm, s2_hbm,
    pred_ref, u1_ref, u2_ref,
    x_ref, t_ref, k1_ref, k2_ref, m1_ref, m2_ref, s1_ref, s2_ref, ls, X, H, E, E1, A1, TG, TS, PS, WG, W1, W2, WB, P1, P2, R, Z, TT, Q, A,
    hs, hr, ws, wr, gs, gr, zs, zr, qs, qr,
):
    gy = lax.axis_index("gy")
    gz = lax.axis_index("gz")
    fs = lax.axis_index("fsdp")
    core = gy % 2
    place = gy * GZ + gz
    tile = (gy // 2) * GZ + gz
    lane = lax.broadcasted_iota(jnp.int32, (C, XL), 1)

    loads = [
        pltpu.make_async_copy(source, ref, ls.at[n])
        for n, (source, ref) in enumerate((
            (k1_hbm, k1_ref), (x_hbm, x_ref), (k2_hbm, k2_ref), (t_hbm, t_ref),
            (m1_hbm, m1_ref), (s1_hbm, s1_ref), (m2_hbm, m2_ref), (s2_hbm, s2_ref),
        ))
    ]
    owed = {}

    def settle(name):
        owed.pop(name)()

    def finish():
        for name in list(owed):
            settle(name)

    for n, load in enumerate(loads):
        load.start()
        owed["load", n] = load.wait
    def plane_device(index):
        return (index // GZ, index % GZ, fs)

    barrier = pltpu.get_barrier_semaphore()

    def greet(n, carry):
        pl.semaphore_signal(
            barrier, inc=1, device_id=plane_device((place + n) % PLANE), device_id_type=MESH
        )
        return carry

    lax.fori_loop(1, PLANE, greet, 0)
    for n in range(1, NF):
        pl.semaphore_signal(
            barrier, inc=1, device_id=(gy, gz, (fs + n) % NF), device_id_type=MESH
        )

    for k, ref in enumerate((k1_ref, k2_ref)):
        settle(("load", 2 * k))
        WG[k, fs] = jnp.zeros((C, 384), bf16)
        WG[k, fs, :, 0:COLS] = ref[...].astype(bf16)
    settle(("load", 1))
    for y in range(TY):
        TS[y] = x_ref[:, y].astype(f32).reshape(C * TZ, XL)
        for z in range(TZ):
            X[y + 2, z + 2] = TS[y, pl.ds(z, C, stride=TZ), :].astype(bf16)

    send_ok = [
        jnp.logical_and(inside(gy + dy, GY), inside(gz + dz, GZ)) for dy, dz in DIRS
    ]
    recv_ok = [
        jnp.logical_and(inside(gy - dy, GY), inside(gz - dz, GZ)) for dy, dz in DIRS
    ]

    def clear_outside(buf, width):
        for d, (dy, dz) in enumerate(DIRS):
            @pl.when(jnp.logical_not(recv_ok[d]))
            def _():
                region = buf.at[edge(dy, TY, width, False), edge(dz, TZ, width, False)]
                region[...] = jnp.zeros(region.shape, bf16)

    clear_outside(X, 2)
    clear_outside(E, 1)

    def halo(buf, width, phase, d):
        dy, dz = DIRS[d]
        return pltpu.make_async_remote_copy(
            src_ref=buf.at[edge(dy, TY, width, True), edge(dz, TZ, width, True)],
            dst_ref=buf.at[edge(dy, TY, width, False), edge(dz, TZ, width, False)],
            send_sem=hs.at[phase, d],
            recv_sem=hr.at[phase, d],
            device_id=(
                jnp.clip(gy + dy, 0, GY - 1), jnp.clip(gz + dz, 0, GZ - 1), fs
            ),
            device_id_type=MESH,
        )

    def halo_start(buf, width, phase, dirs=range(8)):
        def arrived():
            for d in range(8):
                @pl.when(recv_ok[d])
                def _():
                    halo(buf, width, phase, d).wait_recv()

        def sent():
            for d in range(8):
                @pl.when(send_ok[d])
                def _():
                    halo(buf, width, phase, d).wait_send()

        for d in dirs:
            @pl.when(send_ok[d])
            def _():
                halo(buf, width, phase, d).start()
        owed["halo", phase], owed["halo sent", phase] = arrived, sent

    def weight(k, n, owner):
        return pltpu.make_async_remote_copy(
            src_ref=WG.at[k, owner],
            dst_ref=WG.at[k, owner],
            send_sem=ws.at[k, n - 1],
            recv_sem=wr.at[k, n - 1],
            device_id=(gy, gz, (fs + n) % NF),
            device_id_type=MESH,
        )

    def weight_start(k):
        def arrived():
            for n in range(1, NF):
                weight(k, n, (fs - n + NF) % NF).wait_recv()

        def sent():
            for n in range(1, NF):
                weight(k, n, fs).wait_send()

        for n in range(1, NF):
            weight(k, n, fs).start()
        owed["weight", k], owed["weight sent", k] = arrived, sent

    pl.semaphore_wait(barrier, PLANE - 1 + NF - 1)

    weight_start(0)
    halo_start(X, 2, 0)
    weight_start(1)

    settle(("load", 3))
    for y in range(TY):
        TS[y] = t_ref[:, y].astype(f32).reshape(C * TZ, XL)
        for z in range(TZ):
            TG[y, z] = TS[y, pl.ds(z, C, stride=TZ), :]

    def gathered(k):
        return jnp.concatenate([WG[k, f].astype(f32)[:, :COLS] for f in range(NF)], 1)

    def forward_matrix(full, out):
        for dx in range(3):
            out[dx * C:dx * C + C, :] = jnp.concatenate(
                [full[:, (3 * g + dx) * C:(3 * g + dx + 1) * C] for g in range(9)], 1
            ).astype(bf16)

    settle(("weight", 0))
    forward_matrix(gathered(0), W1)

    def conv(w, buf, width, cells, back=False):
        out = jnp.dot(w[...], rows9(buf, width, cells), preferred_element_type=f32)
        res = []
        for h in range(len(cells)):
            q = out[:, h * XL:(h + 1) * XL]
            low, mid, high = q[:C], q[C:2 * C], q[2 * C:]
            if back:
                low, high = high, low
            res.append(mid + roll_right(low, lane) + roll_left(high, lane))
        return zip(cells, res)

    settle(("halo", 0))
    for cells in WIDE:
        for (y, z), a1 in conv(W1, X, 2, cells):
            if 0 <= y < TY and 0 <= z < TZ:
                A1[y, z] = a1
            H[y + 1, z + 1] = jnp.maximum(a1, 0.0).astype(bf16)
    clear_outside(H, 1)

    settle(("weight", 1))
    full2 = gathered(1)
    forward_matrix(full2, W2)

    def conv2(groups):
        for cells in groups:
            for (y, z), a2 in conv(W2, H, 1, cells):
                total = X[y + 2, z + 2].astype(f32) + a2
                PS[y, pl.ds(z, C, stride=TZ), :] = total
                E[y + 1, z + 1] = (total - TG[y, z]).astype(bf16)

    conv2(LOW)
    halo_start(E, 1, 1, (0, 1, 2))
    conv2(HIGH)
    halo_start(E, 1, 1, (3, 4, 5))
    conv2(SIDES)
    halo_start(E, 1, 1, (6, 7))
    conv2(INNER)

    def shifted(e):
        v = e.astype(f32)
        return jnp.concatenate(
            [roll_left(v, lane).astype(bf16), e, roll_right(v, lane).astype(bf16)], 0
        )

    def weight_grad(buf, width, err):
        grad = jnp.zeros((K9, C3), f32)
        for cells in PLANES:
            right = jnp.concatenate([shifted(err(y, z)) for y, z in cells], 1)
            grad += lax.dot_general(
                rows9(buf, width, cells), right, (((1,), (1,)), ((), ())),
                preferred_element_type=f32,
            )
        return grad.T

    def pack(grad, out):
        for f in range(NF):
            pieces = []
            for third in range(3):
                col = COLS * f
                while col < COLS * (f + 1):
                    block, i = col // C, col % C
                    width = min(C - i, COLS * (f + 1) - col)
                    g, dx = block // 3, block % 3
                    pieces.append(
                        grad[dx * C + 16 * third:dx * C + 16 * third + 16,
                             g * C + i:g * C + i + width]
                    )
                    col += width
            pieces.append(jnp.zeros((16, 1024 - 3 * COLS), f32))
            flat = jnp.concatenate(pieces, 1)
            for t in range(16):
                out[t, f] = flat[(t // 8) * 8:(t // 8) * 8 + 8, (t % 8) * 128:(t % 8 + 1) * 128]

    def scatter(k, src):
        def send(n, carry):
            to = (tile + n) % 16
            owner = (2 * (to // GZ) + k) * GZ + to % GZ
            pltpu.make_async_remote_copy(
                src_ref=src.at[to],
                dst_ref=R.at[(place - owner + PLANE) % PLANE],
                send_sem=gs.at[k],
                recv_sem=gr,
                device_id=plane_device(owner),
                device_id_type=MESH,
            ).start()
            return carry

        @pl.when(core == k)
        def _():
            R[0] = src[tile]

        @pl.when(core != k)
        def _():
            send(0, 0)

        lax.fori_loop(1, 16, send, 0)

        def sent():
            for count, mine in ((15, core == k), (16, core != k)):
                @pl.when(mine)
                def _():
                    pltpu.make_async_remote_copy(
                        src_ref=src.at[pl.ds(0, count)], dst_ref=R.at[pl.ds(0, count)],
                        send_sem=gs.at[k], recv_sem=gr, device_id=plane_device(place),
                        device_id_type=MESH,
                    ).wait_send()

        def parts():
            @pl.when(core == k)
            def _():
                pltpu.make_async_remote_copy(
                    src_ref=R.at[pl.ds(1, PLANE - 1)], dst_ref=R.at[pl.ds(1, PLANE - 1)],
                    send_sem=gs.at[k], recv_sem=gr, device_id=plane_device(place),
                    device_id_type=MESH,
                ).wait_recv()

        owed["parts", k], owed["scatter sent", k] = parts, sent

    grad2 = weight_grad(H, 1, lambda y, z: E[y + 1, z + 1])
    pack(grad2, P2)
    scatter(1, P2)

    turned = full2.T
    for dx in range(3):
        WB[dx * C:dx * C + C, :] = jnp.concatenate(
            [
                turned[(26 - 3 * g - 2 + dx) * C:(26 - 3 * g - 2 + dx + 1) * C, :]
                for g in range(9)
            ],
            1,
        ).astype(bf16)

    def back(groups):
        for cells in groups:
            for (y, z), b in conv(WB, E, 1, cells, True):
                E1[y, z] = jnp.where(A1[y, z] > 0, b, 0.0).astype(bf16)

    back(INNER)
    settle(("halo", 1))
    back(LOW + HIGH + SIDES)
    grad1 = weight_grad(X, 2, lambda y, z: E1[y, z])
    pack(grad1, P1)
    scatter(0, P1)

    for y in range(TY):
        pred_ref[:, y] = PS[y].reshape(C, TZ, XL).astype(bf16)

    settle(("parts", 1))
    settle(("parts", 0))
    own = R[0]
    for n in range(1, PLANE):
        own = own + R[n]
    Z[fs] = own

    def along(n, owner):
        return pltpu.make_async_remote_copy(
            src_ref=Z.at[owner], dst_ref=Z.at[owner], send_sem=zs.at[n - 1],
            recv_sem=zr.at[n - 1], device_id=(gy, gz, (fs + n) % NF), device_id_type=MESH,
        )

    def sums():
        for n in range(1, NF):
            along(n, (fs - n + NF) % NF).wait_recv()

    def sums_sent():
        for n in range(1, NF):
            along(n, fs).wait_send()

    for n in range(1, NF):
        along(n, fs).start()
    owed["sums"], owed["sums sent"] = sums, sums_sent
    settle("sums")
    total = Z[0] + Z[1] + Z[2] + Z[3]
    TT[...] = total
    Q[0] = TT[fs]
    Q[1] = jnp.sum(total * total, 0)

    slot = core * 16 + tile
    A[slot] = Q[...]

    def spread(n, carry):
        pltpu.make_async_remote_copy(
            src_ref=Q, dst_ref=A.at[slot], send_sem=qs, recv_sem=qr,
            device_id=plane_device((place + n) % PLANE), device_id_type=MESH,
        ).start()
        return carry

    lax.fori_loop(1, PLANE, spread, 0)
    gather = pltpu.make_async_remote_copy(
        src_ref=A.at[pl.ds(0, PLANE - 1)], dst_ref=A.at[pl.ds(0, PLANE - 1)],
        send_sem=qs, recv_sem=qr, device_id=plane_device(place), device_id_type=MESH,
    )
    owed["gather"], owed["gather sent"] = gather.wait_recv, gather.wait_send
    settle("gather")

    squares = A[0, 1]
    for n in range(1, PLANE):
        squares = squares + A[n, 1]
    norm = jnp.sqrt(jnp.sum(squares, keepdims=True))
    factor = jnp.minimum(1.0, 1.0 / (norm + 1e-06))
    for n in range(4, 8):
        settle(("load", n))
    for k, (m_ref, s_ref, u_ref) in enumerate(
        ((m1_ref, s1_ref, u1_ref), (m2_ref, s2_ref, u2_ref))
    ):
        flat = jnp.concatenate(
            [
                jnp.concatenate([A[k * 16 + r * 8 + t, 0] for t in range(8)], 1)
                for r in range(2)
            ],
            0,
        )
        for third in range(3):
            at = pl.ds(16 * third, 16)
            grad = factor * flat[:, COLS * third:COLS * (third + 1)]
            first = 0.9 * m_ref[at, :] + 0.1 * grad
            second = 0.999 * s_ref[at, :] + 0.001 * grad * grad
            u_ref[at, :] = first / first_bias / (jnp.sqrt(second / second_bias) + 1e-08)

    finish()


def hand_on(*refs):
    copies = [
        pltpu.make_async_copy(refs[n], refs[3 + n], refs[6].at[n]) for n in range(3)
    ]
    for copy in copies:
        copy.start()
    for copy in copies:
        copy.wait()


def shards(
    coarse_field, fine_target, kernel_one, kernel_two,
    moment_one, moment_two, second_one, second_two,
):
    hbm = pl.BlockSpec(memory_space=pltpu.HBM)
    vmem = pl.BlockSpec(memory_space=pltpu.VMEM)
    dma = pltpu.SemaphoreType.DMA
    padded = [pltpu.VMEM((TY + 2 * w, TZ + 2 * w, C, XL), bf16) for w in (2, 1, 1)]
    results = [
        jax.ShapeDtypeStruct((C, TY, TZ, XL), bf16),
        jax.ShapeDtypeStruct((C, COLS), f32),
        jax.ShapeDtypeStruct((C, COLS), f32),
    ]
    computed = pl.pallas_call(
        kernel,
        out_shape=[pltpu.VMEM(r.shape, r.dtype) for r in results],
        in_specs=[hbm] * 8,
        out_specs=[vmem] * 3,
        scratch_shapes=[
            pltpu.VMEM((C, TY, TZ, XL), bf16), pltpu.VMEM((C, TY, TZ, XL), bf16),
        ] + [pltpu.VMEM((C, COLS), f32)] * 6 + [
            dma((8,)),
            *padded,
            pltpu.VMEM((TY, TZ, C, XL), bf16),
            pltpu.VMEM((TY, TZ, C, XL), f32),
            pltpu.VMEM((TY, TZ, C, XL), f32),
            pltpu.VMEM((TY, C * TZ, XL), f32),
            pltpu.VMEM((TY, C * TZ, XL), f32),
            pltpu.VMEM((2, NF, C, 384), bf16),
            pltpu.VMEM((C3, K9), bf16),
            pltpu.VMEM((C3, K9), bf16),
            pltpu.VMEM((C3, K9), bf16),
            pltpu.VMEM((16, NF, 8, 128), f32),
            pltpu.VMEM((16, NF, 8, 128), f32),
            pltpu.VMEM((PLANE, NF, 8, 128), f32),
            pltpu.VMEM((NF, NF, 8, 128), f32),
            pltpu.VMEM((NF, 8, 128), f32),
            pltpu.VMEM((2, 8, 128), f32),
            pltpu.VMEM((PLANE, 2, 8, 128), f32),
            dma((2, 8)), dma((2, 8)),
            dma((2, 3)), dma((2, 3)),
            dma((2,)), dma,
            dma((3,)), dma((3,)),
            dma, dma,
        ],
        compiler_params=pltpu.CompilerParams(
            collective_id=0, has_side_effects=True, vmem_limit_bytes=60 << 20
        ),
    )(
        coarse_field[0], fine_target[0], kernel_one, kernel_two,
        moment_one, moment_two, second_one, second_two,
    )
    prediction, update_one, update_two = pl.pallas_call(
        hand_on,
        out_shape=results,
        in_specs=[vmem] * 3,
        out_specs=[hbm] * 3,
        scratch_shapes=[dma((3,))],
        compiler_params=pltpu.CompilerParams(vmem_limit_bytes=4 << 20),
    )(*computed)
    return prediction[None], update_one, update_two


def solution(mesh):
    field = P("fsdp", None, "gy", "gz", None)
    state = P(None, "fsdp")
    return jax.shard_map(
        shards,
        mesh=mesh,
        in_specs=(field, field) + (state,) * 6,
        out_specs=(field, state, state),
        check_vma=False,
    )
```

```python
import jax
import jax.numpy as jnp
from jax import lax
from jax.experimental import pallas as pl
from jax.experimental.pallas import tpu as pltpu
from jax.sharding import PartitionSpec as P

first_bias = 0.9999734386011124
second_bias = 0.09520785288629038

C = 48
TY, TZ, XL = 4, 8, 128
GY, GZ, NF = 4, 8, 4
PLANE = GY * GZ
TAPS = 27 * C
COLS = TAPS // NF
K9 = 9 * C
C3 = 3 * C
MESH = pl.DeviceIdType.MESH
f32, bf16 = jnp.float32, jnp.bfloat16
DIRS = [(-1, -1), (-1, 1), (-1, 0), (1, -1), (1, 1), (1, 0), (0, -1), (0, 1)]


def edge(step, size, width, sending):
    if step == 0:
        return pl.ds(width, size)
    if sending:
        return pl.ds(width if step < 0 else size, width)
    return pl.ds(size + width if step < 0 else 0, width)


def inside(value, count):
    return jnp.logical_and(value >= 0, value < count)


def roll_right(v, lane):
    return jnp.where(lane > 0, pltpu.roll(v, 1, 1), 0.0)


def roll_left(v, lane):
    return jnp.where(lane < XL - 1, pltpu.roll(v, XL - 1, 1), 0.0)


def rows9(buf, width, cells):
    off = width - 1
    return jnp.concatenate(
        [
            jnp.concatenate(
                [buf[y + dy + off, z + off:z + off + 3].reshape(C3, XL) for y, z in cells], 1
            )
            for dy in range(3)
        ],
        0,
    )


LOW = [((0, z), (0, z + 1)) for z in range(0, TZ, 2)]
HIGH = [((TY - 1, z), (TY - 1, z + 1)) for z in range(0, TZ, 2)]
SIDES = [((y, 0), (y, TZ - 1)) for y in range(1, TY - 1)]
INNER = [((y, z), (y, z + 1)) for y in range(1, TY - 1) for z in range(1, TZ - 1, 2)]
WIDE = [((y, z), (y, z + 1)) for y in range(-1, TY + 1) for z in range(-1, TZ + 1, 2)]
PLANES = [tuple((y, z) for z in range(TZ)) for y in range(TY)]


def kernel(
    x_hbm, t_hbm, k1_hbm, k2_hbm, m1_hbm, m2_hbm, s1_hbm, s2_hbm,
    pred_ref, u1_ref, u2_ref,
    x_ref, t_ref, k1_ref, k2_ref, m1_ref, m2_ref, s1_ref, s2_ref, ls, X, H, E, E1, A1, TG, TS, PS, WG, W1, W2, WB, P1, P2, R, Z, TT, Q, A,
    hs, hr, ws, wr, gs, gr, zs, zr, qs, qr,
):
    gy = lax.axis_index("gy")
    gz = lax.axis_index("gz")
    fs = lax.axis_index("fsdp")
    core = gy % 2
    place = gy * GZ + gz
    tile = (gy // 2) * GZ + gz
    lane = lax.broadcasted_iota(jnp.int32, (C, XL), 1)

    loads = [
        pltpu.make_async_copy(source, ref, ls.at[n])
        for n, (source, ref) in enumerate((
            (k1_hbm, k1_ref), (x_hbm, x_ref), (k2_hbm, k2_ref), (t_hbm, t_ref),
            (m1_hbm, m1_ref), (s1_hbm, s1_ref), (m2_hbm, m2_ref), (s2_hbm, s2_ref),
        ))
    ]
    owed = {}

    def settle(name):
        owed.pop(name)()

    def finish():
        for name in list(owed):
            settle(name)

    for n, load in enumerate(loads):
        load.start()
        owed["load", n] = load.wait
    def plane_device(index):
        return (index // GZ, index % GZ, fs)

    barrier = pltpu.get_barrier_semaphore()

    def greet(n, carry):
        pl.semaphore_signal(
            barrier, inc=1, device_id=plane_device((place + n) % PLANE), device_id_type=MESH
        )
        return carry

    lax.fori_loop(1, PLANE, greet, 0)
    for n in range(1, NF):
        pl.semaphore_signal(
            barrier, inc=1, device_id=(gy, gz, (fs + n) % NF), device_id_type=MESH
        )

    for k, ref in enumerate((k1_ref, k2_ref)):
        settle(("load", 2 * k))
        WG[k, fs] = jnp.zeros((C, 384), bf16)
        WG[k, fs, :, 0:COLS] = ref[...].astype(bf16)
    settle(("load", 1))
    for y in range(TY):
        TS[y] = x_ref[:, y].astype(f32).reshape(C * TZ, XL)
        for z in range(TZ):
            X[y + 2, z + 2] = TS[y, pl.ds(z, C, stride=TZ), :].astype(bf16)

    send_ok = [
        jnp.logical_and(inside(gy + dy, GY), inside(gz + dz, GZ)) for dy, dz in DIRS
    ]
    recv_ok = [
        jnp.logical_and(inside(gy - dy, GY), inside(gz - dz, GZ)) for dy, dz in DIRS
    ]

    def clear_outside(buf, width):
        for d, (dy, dz) in enumerate(DIRS):
            @pl.when(jnp.logical_not(recv_ok[d]))
            def _():
                region = buf.at[edge(dy, TY, width, False), edge(dz, TZ, width, False)]
                region[...] = jnp.zeros(region.shape, bf16)

    clear_outside(X, 2)
    clear_outside(E, 1)

    def halo(buf, width, phase, d):
        dy, dz = DIRS[d]
        return pltpu.make_async_remote_copy(
            src_ref=buf.at[edge(dy, TY, width, True), edge(dz, TZ, width, True)],
            dst_ref=buf.at[edge(dy, TY, width, False), edge(dz, TZ, width, False)],
            send_sem=hs.at[phase, d],
            recv_sem=hr.at[phase, d],
            device_id=(
                jnp.clip(gy + dy, 0, GY - 1), jnp.clip(gz + dz, 0, GZ - 1), fs
            ),
            device_id_type=MESH,
        )

    def halo_start(buf, width, phase, dirs=range(8)):
        def arrived():
            for d in range(8):
                @pl.when(recv_ok[d])
                def _():
                    halo(buf, width, phase, d).wait_recv()

        def sent():
            for d in range(8):
                @pl.when(send_ok[d])
                def _():
                    halo(buf, width, phase, d).wait_send()

        for d in dirs:
            @pl.when(send_ok[d])
            def _():
                halo(buf, width, phase, d).start()
        owed["halo", phase], owed["halo sent", phase] = arrived, sent

    def weight(k, n, owner):
        return pltpu.make_async_remote_copy(
            src_ref=WG.at[k, owner],
            dst_ref=WG.at[k, owner],
            send_sem=ws.at[k, n - 1],
            recv_sem=wr.at[k, n - 1],
            device_id=(gy, gz, (fs + n) % NF),
            device_id_type=MESH,
        )

    def weight_start(k):
        def arrived():
            for n in range(1, NF):
                weight(k, n, (fs - n + NF) % NF).wait_recv()

        def sent():
            for n in range(1, NF):
                weight(k, n, fs).wait_send()

        for n in range(1, NF):
            weight(k, n, fs).start()
        owed["weight", k], owed["weight sent", k] = arrived, sent

    pl.semaphore_wait(barrier, PLANE - 1 + NF - 1)

    weight_start(0)
    halo_start(X, 2, 0)
    weight_start(1)

    settle(("load", 3))
    for y in range(TY):
        TS[y] = t_ref[:, y].astype(f32).reshape(C * TZ, XL)
        for z in range(TZ):
            TG[y, z] = TS[y, pl.ds(z, C, stride=TZ), :]

    def gathered(k):
        return jnp.concatenate([WG[k, f].astype(f32)[:, :COLS] for f in range(NF)], 1)

    def forward_matrix(full, out):
        for dx in range(3):
            out[dx * C:dx * C + C, :] = jnp.concatenate(
                [full[:, (3 * g + dx) * C:(3 * g + dx + 1) * C] for g in range(9)], 1
            ).astype(bf16)

    settle(("weight", 0))
    forward_matrix(gathered(0), W1)

    def conv(w, buf, width, cells, back=False):
        out = jnp.dot(w[...], rows9(buf, width, cells), preferred_element_type=f32)
        res = []
        for h in range(len(cells)):
            q = out[:, h * XL:(h + 1) * XL]
            low, mid, high = q[:C], q[C:2 * C], q[2 * C:]
            if back:
                low, high = high, low
            res.append(mid + roll_right(low, lane) + roll_left(high, lane))
        return zip(cells, res)

    settle(("halo", 0))
    for cells in WIDE:
        for (y, z), a1 in conv(W1, X, 2, cells):
            if 0 <= y < TY and 0 <= z < TZ:
                A1[y, z] = a1
            H[y + 1, z + 1] = jnp.maximum(a1, 0.0).astype(bf16)
    clear_outside(H, 1)

    settle(("weight", 1))
    full2 = gathered(1)
    forward_matrix(full2, W2)

    def conv2(groups):
        for cells in groups:
            for (y, z), a2 in conv(W2, H, 1, cells):
                total = X[y + 2, z + 2].astype(f32) + a2
                PS[y, pl.ds(z, C, stride=TZ), :] = total
                E[y + 1, z + 1] = (total - TG[y, z]).astype(bf16)

    conv2(LOW)
    halo_start(E, 1, 1, (0, 1, 2))
    conv2(HIGH)
    halo_start(E, 1, 1, (3, 4, 5))
    conv2(SIDES)
    halo_start(E, 1, 1, (6, 7))
    conv2(INNER)

    def shifted(e):
        v = e.astype(f32)
        return jnp.concatenate(
            [roll_left(v, lane).astype(bf16), e, roll_right(v, lane).astype(bf16)], 0
        )

    def weight_grad(buf, width, err):
        grad = jnp.zeros((K9, C3), f32)
        for cells in PLANES:
            right = jnp.concatenate([shifted(err(y, z)) for y, z in cells], 1)
            grad += lax.dot_general(
                rows9(buf, width, cells), right, (((1,), (1,)), ((), ())),
                preferred_element_type=f32,
            )
        return grad.T

    def pack(grad, out):
        shares = []
        for f in range(NF):
            pieces = []
            for third in range(3):
                col = COLS * f
                while col < COLS * (f + 1):
                    block, i = col // C, col % C
                    width = min(C - i, COLS * (f + 1) - col)
                    g, dx = block // 3, block % 3
                    pieces.append(
                        grad[dx * C + 16 * third:dx * C + 16 * third + 16,
                             g * C + i:g * C + i + width]
                    )
                    col += width
            pieces.append(jnp.zeros((16, 1024 - 3 * COLS), f32))
            flat = jnp.concatenate(pieces, 1)
            shares.append(flat)
        for t in range(16):
            at = (slice((t // 8) * 8, (t // 8) * 8 + 8), slice((t % 8) * 128, (t % 8 + 1) * 128))
            out[t] = jnp.concatenate([flat[at] for flat in shares], 0).astype(bf16)

    def scatter(k, src):
        def send(n, carry):
            to = (tile + n) % 16
            owner = (2 * (to // GZ) + k) * GZ + to % GZ
            pltpu.make_async_remote_copy(
                src_ref=src.at[to],
                dst_ref=R.at[(place - owner + PLANE) % PLANE],
                send_sem=gs.at[k],
                recv_sem=gr,
                device_id=plane_device(owner),
                device_id_type=MESH,
            ).start()
            return carry

        @pl.when(core == k)
        def _():
            R[0] = src[tile]

        @pl.when(core != k)
        def _():
            send(0, 0)

        lax.fori_loop(1, 16, send, 0)

        def sent():
            for count, mine in ((15, core == k), (16, core != k)):
                @pl.when(mine)
                def _():
                    pltpu.make_async_remote_copy(
                        src_ref=src.at[pl.ds(0, count)], dst_ref=R.at[pl.ds(0, count)],
                        send_sem=gs.at[k], recv_sem=gr, device_id=plane_device(place),
                        device_id_type=MESH,
                    ).wait_send()

        def parts():
            @pl.when(core == k)
            def _():
                pltpu.make_async_remote_copy(
                    src_ref=R.at[pl.ds(1, PLANE - 1)], dst_ref=R.at[pl.ds(1, PLANE - 1)],
                    send_sem=gs.at[k], recv_sem=gr, device_id=plane_device(place),
                    device_id_type=MESH,
                ).wait_recv()

        owed["parts", k], owed["scatter sent", k] = parts, sent

    grad2 = weight_grad(H, 1, lambda y, z: E[y + 1, z + 1])
    pack(grad2, P2)
    scatter(1, P2)

    turned = full2.T
    for dx in range(3):
        WB[dx * C:dx * C + C, :] = jnp.concatenate(
            [
                turned[(26 - 3 * g - 2 + dx) * C:(26 - 3 * g - 2 + dx + 1) * C, :]
                for g in range(9)
            ],
            1,
        ).astype(bf16)

    def back(groups):
        for cells in groups:
            for (y, z), b in conv(WB, E, 1, cells, True):
                E1[y, z] = jnp.where(A1[y, z] > 0, b, 0.0).astype(bf16)

    back(INNER)
    settle(("halo", 1))
    back(LOW + HIGH + SIDES)
    grad1 = weight_grad(X, 2, lambda y, z: E1[y, z])
    pack(grad1, P1)
    scatter(0, P1)

    for y in range(TY):
        pred_ref[:, y] = PS[y].reshape(C, TZ, XL).astype(bf16)

    settle(("parts", 1))
    settle(("parts", 0))
    own = R[0].astype(f32)
    for n in range(1, PLANE):
        own = own + R[n].astype(f32)
    Z[fs] = own.reshape(NF, 8, 128)

    def along(n, owner):
        return pltpu.make_async_remote_copy(
            src_ref=Z.at[owner], dst_ref=Z.at[owner], send_sem=zs.at[n - 1],
            recv_sem=zr.at[n - 1], device_id=(gy, gz, (fs + n) % NF), device_id_type=MESH,
        )

    def sums():
        for n in range(1, NF):
            along(n, (fs - n + NF) % NF).wait_recv()

    def sums_sent():
        for n in range(1, NF):
            along(n, fs).wait_send()

    for n in range(1, NF):
        along(n, fs).start()
    owed["sums"], owed["sums sent"] = sums, sums_sent
    settle("sums")
    total = Z[0] + Z[1] + Z[2] + Z[3]
    TT[...] = total
    squares = jnp.sum(jnp.sum(total * total, 0), 0, keepdims=True)
    rounded = squares.astype(bf16).astype(f32)
    Q[...] = jnp.concatenate(
        [TT[fs], rounded, squares - rounded, jnp.zeros((6, 128), f32)], 0
    ).astype(bf16)

    slot = core * 16 + tile
    A[slot] = Q[...]

    def spread(n, carry):
        pltpu.make_async_remote_copy(
            src_ref=Q, dst_ref=A.at[slot], send_sem=qs, recv_sem=qr,
            device_id=plane_device((place + n) % PLANE), device_id_type=MESH,
        ).start()
        return carry

    lax.fori_loop(1, PLANE, spread, 0)
    gather = pltpu.make_async_remote_copy(
        src_ref=A.at[pl.ds(0, PLANE - 1)], dst_ref=A.at[pl.ds(0, PLANE - 1)],
        send_sem=qs, recv_sem=qr, device_id=plane_device(place), device_id_type=MESH,
    )
    owed["gather"], owed["gather sent"] = gather.wait_recv, gather.wait_send
    settle("gather")

    tiles = [A[n].astype(f32) for n in range(PLANE)]
    squares = tiles[0][8:]
    for tile_in in tiles[1:]:
        squares = squares + tile_in[8:]
    norm = jnp.sqrt(jnp.sum(squares, keepdims=True))
    factor = jnp.minimum(1.0, 1.0 / (norm + 1e-06))
    for n in range(4, 8):
        settle(("load", n))
    for k, (m_ref, s_ref, u_ref) in enumerate(
        ((m1_ref, s1_ref, u1_ref), (m2_ref, s2_ref, u2_ref))
    ):
        flat = jnp.concatenate(
            [
                jnp.concatenate([tiles[k * 16 + r * 8 + t][:8] for t in range(8)], 1)
                for r in range(2)
            ],
            0,
        )
        for third in range(3):
            at = pl.ds(16 * third, 16)
            grad = factor * flat[:, COLS * third:COLS * (third + 1)]
            first = 0.9 * m_ref[at, :] + 0.1 * grad
            second = 0.999 * s_ref[at, :] + 0.001 * grad * grad
            u_ref[at, :] = first / first_bias / (jnp.sqrt(second / second_bias) + 1e-08)

    finish()


def hand_on(*refs):
    copies = [
        pltpu.make_async_copy(refs[n], refs[3 + n], refs[6].at[n]) for n in range(3)
    ]
    for copy in copies:
        copy.start()
    for copy in copies:
        copy.wait()


def shards(
    coarse_field, fine_target, kernel_one, kernel_two,
    moment_one, moment_two, second_one, second_two,
):
    hbm = pl.BlockSpec(memory_space=pltpu.HBM)
    vmem = pl.BlockSpec(memory_space=pltpu.VMEM)
    dma = pltpu.SemaphoreType.DMA
    padded = [pltpu.VMEM((TY + 2 * w, TZ + 2 * w, C, XL), bf16) for w in (2, 1, 1)]
    results = [
        jax.ShapeDtypeStruct((C, TY, TZ, XL), bf16),
        jax.ShapeDtypeStruct((C, COLS), f32),
        jax.ShapeDtypeStruct((C, COLS), f32),
    ]
    computed = pl.pallas_call(
        kernel,
        out_shape=[pltpu.VMEM(r.shape, r.dtype) for r in results],
        in_specs=[hbm] * 8,
        out_specs=[vmem] * 3,
        scratch_shapes=[
            pltpu.VMEM((C, TY, TZ, XL), bf16), pltpu.VMEM((C, TY, TZ, XL), bf16),
        ] + [pltpu.VMEM((C, COLS), f32)] * 6 + [
            dma((8,)),
            *padded,
            pltpu.VMEM((TY, TZ, C, XL), bf16),
            pltpu.VMEM((TY, TZ, C, XL), f32),
            pltpu.VMEM((TY, TZ, C, XL), f32),
            pltpu.VMEM((TY, C * TZ, XL), f32),
            pltpu.VMEM((TY, C * TZ, XL), f32),
            pltpu.VMEM((2, NF, C, 384), bf16),
            pltpu.VMEM((C3, K9), bf16),
            pltpu.VMEM((C3, K9), bf16),
            pltpu.VMEM((C3, K9), bf16),
            pltpu.VMEM((16, NF * 8, 128), bf16),
            pltpu.VMEM((16, NF * 8, 128), bf16),
            pltpu.VMEM((PLANE, NF * 8, 128), bf16),
            pltpu.VMEM((NF, NF, 8, 128), f32),
            pltpu.VMEM((NF, 8, 128), f32),
            pltpu.VMEM((16, 128), bf16),
            pltpu.VMEM((PLANE, 16, 128), bf16),
            dma((2, 8)), dma((2, 8)),
            dma((2, 3)), dma((2, 3)),
            dma((2,)), dma,
            dma((3,)), dma((3,)),
            dma, dma,
        ],
        compiler_params=pltpu.CompilerParams(
            collective_id=0, has_side_effects=True, vmem_limit_bytes=60 << 20
        ),
    )(
        coarse_field[0], fine_target[0], kernel_one, kernel_two,
        moment_one, moment_two, second_one, second_two,
    )
    prediction, update_one, update_two = pl.pallas_call(
        hand_on,
        out_shape=results,
        in_specs=[vmem] * 3,
        out_specs=[hbm] * 3,
        scratch_shapes=[dma((3,))],
        compiler_params=pltpu.CompilerParams(vmem_limit_bytes=4 << 20),
    )(*computed)
    return prediction[None], update_one, update_two


def solution(mesh):
    field = P("fsdp", None, "gy", "gz", None)
    state = P(None, "fsdp")
    return jax.shard_map(
        shards,
        mesh=mesh,
        in_specs=(field, field) + (state,) * 6,
        out_specs=(field, state, state),
        check_vma=False,
    )
```

```python
import jax
import jax.numpy as jnp
from jax import lax
from jax.experimental import pallas as pl
from jax.experimental.pallas import tpu as pltpu
from jax.sharding import PartitionSpec as P

first_bias = 0.9999734386011124
second_bias = 0.09520785288629038

C = 48
TY, TZ, XL = 4, 8, 128
GY, GZ, NF = 4, 8, 4
PLANE = GY * GZ
TAPS = 27 * C
COLS = TAPS // NF
K9 = 9 * C
C3 = 3 * C
MESH = pl.DeviceIdType.MESH
f32, bf16 = jnp.float32, jnp.bfloat16
DIRS = [(-1, -1), (-1, 1), (-1, 0), (1, -1), (1, 1), (1, 0), (0, -1), (0, 1)]


def edge(step, size, width, sending):
    if step == 0:
        return pl.ds(width, size)
    if sending:
        return pl.ds(width if step < 0 else size, width)
    return pl.ds(size + width if step < 0 else 0, width)


def inside(value, count):
    return jnp.logical_and(value >= 0, value < count)


def roll_right(v, lane):
    return jnp.where(lane > 0, pltpu.roll(v, 1, 1), 0.0)


def roll_left(v, lane):
    return jnp.where(lane < XL - 1, pltpu.roll(v, XL - 1, 1), 0.0)


def rows9(buf, width, cells):
    off = width - 1
    return jnp.concatenate(
        [
            jnp.concatenate(
                [buf[y + dy + off, z + off:z + off + 3].reshape(C3, XL) for y, z in cells], 1
            )
            for dy in range(3)
        ],
        0,
    )


LOW = [((0, z), (0, z + 1)) for z in range(0, TZ, 2)]
HIGH = [((TY - 1, z), (TY - 1, z + 1)) for z in range(0, TZ, 2)]
SIDES = [((y, 0), (y, TZ - 1)) for y in range(1, TY - 1)]
INNER = [((y, z), (y, z + 1)) for y in range(1, TY - 1) for z in range(1, TZ - 1, 2)]
WIDE = [((y, z), (y, z + 1)) for y in (-1, 0, TY - 1, TY) for z in range(-1, TZ + 1, 2)]
WIDE += [((y, z), (y, z + 1)) for y in range(1, TY - 1) for z in (-1, TZ - 1)]
PLANES = [tuple((y, z) for z in range(TZ)) for y in range(TY)]


def kernel(
    x_hbm, t_hbm, k1_hbm, k2_hbm, m1_hbm, m2_hbm, s1_hbm, s2_hbm,
    pred_ref, u1_ref, u2_ref,
    x_ref, t_ref, k1_ref, k2_ref, m1_ref, m2_ref, s1_ref, s2_ref, ls, X, H, E, E1, A1, TG, TS, PS, WG, W1, W2, WB, G, P1, P2, R, Z, TT, Q, A,
    hs, hr, ws, wr, gs, gr, zs, zr, qs, qr,
):
    gy = lax.axis_index("gy")
    gz = lax.axis_index("gz")
    fs = lax.axis_index("fsdp")
    core = gy % 2
    place = gy * GZ + gz
    tile = (gy // 2) * GZ + gz
    lane = lax.broadcasted_iota(jnp.int32, (C, XL), 1)

    loads = [
        pltpu.make_async_copy(source, ref, ls.at[n])
        for n, (source, ref) in enumerate((
            (k1_hbm, k1_ref), (x_hbm, x_ref), (k2_hbm, k2_ref), (t_hbm, t_ref),
            (m1_hbm, m1_ref), (s1_hbm, s1_ref), (m2_hbm, m2_ref), (s2_hbm, s2_ref),
        ))
    ]
    owed = {}

    def settle(name):
        owed.pop(name)()

    def finish():
        for name in list(owed):
            settle(name)

    for n, load in enumerate(loads):
        load.start()
        owed["load", n] = load.wait
    def plane_device(index):
        return (index // GZ, index % GZ, fs)

    barrier = pltpu.get_barrier_semaphore()

    def greet(n, carry):
        pl.semaphore_signal(
            barrier, inc=1, device_id=plane_device((place + n) % PLANE), device_id_type=MESH
        )
        return carry

    lax.fori_loop(1, PLANE, greet, 0)
    for n in range(1, NF):
        pl.semaphore_signal(
            barrier, inc=1, device_id=(gy, gz, (fs + n) % NF), device_id_type=MESH
        )

    for k, ref in enumerate((k1_ref, k2_ref)):
        settle(("load", 2 * k))
        WG[k, fs] = jnp.zeros((C, 384), bf16)
        WG[k, fs, :, 0:COLS] = ref[...].astype(bf16)
    settle(("load", 1))
    for y in range(TY):
        TS[y] = x_ref[:, y].astype(f32).reshape(C * TZ, XL)
        for z in range(TZ):
            X[y + 2, z + 2] = TS[y, pl.ds(z, C, stride=TZ), :].astype(bf16)

    send_ok = [
        jnp.logical_and(inside(gy + dy, GY), inside(gz + dz, GZ)) for dy, dz in DIRS
    ]
    recv_ok = [
        jnp.logical_and(inside(gy - dy, GY), inside(gz - dz, GZ)) for dy, dz in DIRS
    ]

    def clear_outside(buf, width):
        for d, (dy, dz) in enumerate(DIRS):
            @pl.when(jnp.logical_not(recv_ok[d]))
            def _():
                region = buf.at[edge(dy, TY, width, False), edge(dz, TZ, width, False)]
                region[...] = jnp.zeros(region.shape, bf16)

    clear_outside(X, 2)
    clear_outside(E, 1)

    def halo(buf, width, phase, d):
        dy, dz = DIRS[d]
        return pltpu.make_async_remote_copy(
            src_ref=buf.at[edge(dy, TY, width, True), edge(dz, TZ, width, True)],
            dst_ref=buf.at[edge(dy, TY, width, False), edge(dz, TZ, width, False)],
            send_sem=hs.at[phase, d],
            recv_sem=hr.at[phase, d],
            device_id=(
                jnp.clip(gy + dy, 0, GY - 1), jnp.clip(gz + dz, 0, GZ - 1), fs
            ),
            device_id_type=MESH,
        )

    def halo_start(buf, width, phase, dirs=range(8)):
        def arrived():
            for d in range(8):
                @pl.when(recv_ok[d])
                def _():
                    halo(buf, width, phase, d).wait_recv()

        def sent():
            for d in range(8):
                @pl.when(send_ok[d])
                def _():
                    halo(buf, width, phase, d).wait_send()

        for d in dirs:
            @pl.when(send_ok[d])
            def _():
                halo(buf, width, phase, d).start()
        owed["halo", phase], owed["halo sent", phase] = arrived, sent

    def weight(k, n, owner):
        return pltpu.make_async_remote_copy(
            src_ref=WG.at[k, owner],
            dst_ref=WG.at[k, owner],
            send_sem=ws.at[k, n - 1],
            recv_sem=wr.at[k, n - 1],
            device_id=(gy, gz, (fs + n) % NF),
            device_id_type=MESH,
        )

    def weight_start(k):
        def arrived():
            for n in range(1, NF):
                weight(k, n, (fs - n + NF) % NF).wait_recv()

        def sent():
            for n in range(1, NF):
                weight(k, n, fs).wait_send()

        for n in range(1, NF):
            weight(k, n, fs).start()
        owed["weight", k], owed["weight sent", k] = arrived, sent

    pl.semaphore_wait(barrier, PLANE - 1 + NF - 1)

    weight_start(0)
    halo_start(X, 2, 0)
    weight_start(1)

    settle(("load", 3))
    for y in range(TY):
        TS[y] = t_ref[:, y].astype(f32).reshape(C * TZ, XL)
        for z in range(TZ):
            TG[y, z] = TS[y, pl.ds(z, C, stride=TZ), :]

    def gathered(k):
        return jnp.concatenate([WG[k, f].astype(f32)[:, :COLS] for f in range(NF)], 1)

    def forward_matrix(full, out):
        for dx in range(3):
            out[dx * C:dx * C + C, :] = jnp.concatenate(
                [full[:, (3 * g + dx) * C:(3 * g + dx + 1) * C] for g in range(9)], 1
            ).astype(bf16)

    settle(("weight", 0))
    forward_matrix(gathered(0), W1)

    def conv(w, buf, width, cells, back=False):
        out = jnp.dot(w[...], rows9(buf, width, cells), preferred_element_type=f32)
        res = []
        for h in range(len(cells)):
            q = out[:, h * XL:(h + 1) * XL]
            low, mid, high = q[:C], q[C:2 * C], q[2 * C:]
            if back:
                low, high = high, low
            res.append(mid + roll_right(low, lane) + roll_left(high, lane))
        return zip(cells, res)

    def conv1(groups):
        for cells in groups:
            for (y, z), a1 in conv(W1, X, 2, cells):
                if 0 <= y < TY and 0 <= z < TZ:
                    A1[y, z] = a1
                H[y + 1, z + 1] = jnp.maximum(a1, 0.0).astype(bf16)

    conv1(INNER)
    settle(("weight", 1))
    full2 = gathered(1)
    forward_matrix(full2, W2)
    settle(("halo", 0))
    conv1(WIDE)
    clear_outside(H, 1)

    def conv2(groups):
        for cells in groups:
            for (y, z), a2 in conv(W2, H, 1, cells):
                total = X[y + 2, z + 2].astype(f32) + a2
                PS[y, pl.ds(z, C, stride=TZ), :] = total
                E[y + 1, z + 1] = (total - TG[y, z]).astype(bf16)

    conv2(LOW)
    halo_start(E, 1, 1, (0, 1, 2))
    conv2(HIGH)
    halo_start(E, 1, 1, (3, 4, 5))
    conv2(SIDES)
    halo_start(E, 1, 1, (6, 7))
    conv2(INNER)

    def shifted(e):
        v = e.astype(f32)
        return jnp.concatenate(
            [roll_left(v, lane).astype(bf16), e, roll_right(v, lane).astype(bf16)], 0
        )

    def weight_grad(buf, width, err, groups):
        grad = None
        for cells in groups:
            right = jnp.concatenate([shifted(err(y, z)) for y, z in cells], 1)
            part = lax.dot_general(
                rows9(buf, width, cells), right, (((1,), (1,)), ((), ())),
                preferred_element_type=f32,
            )
            grad = part if grad is None else grad + part
        return grad

    def pack(grad, out):
        grad = grad.T
        shares = []
        for f in range(NF):
            pieces = []
            for third in range(3):
                col = COLS * f
                while col < COLS * (f + 1):
                    block, i = col // C, col % C
                    width = min(C - i, COLS * (f + 1) - col)
                    g, dx = block // 3, block % 3
                    pieces.append(
                        grad[dx * C + 16 * third:dx * C + 16 * third + 16,
                             g * C + i:g * C + i + width]
                    )
                    col += width
            pieces.append(jnp.zeros((16, 1024 - 3 * COLS), f32))
            flat = jnp.concatenate(pieces, 1)
            shares.append(flat)
        for t in range(16):
            at = (slice((t // 8) * 8, (t // 8) * 8 + 8), slice((t % 8) * 128, (t % 8 + 1) * 128))
            out[t] = jnp.concatenate([flat[at] for flat in shares], 0).astype(bf16)

    def scatter(k, src):
        def send(n, carry):
            to = (tile + n) % 16
            owner = (2 * (to // GZ) + k) * GZ + to % GZ
            pltpu.make_async_remote_copy(
                src_ref=src.at[to],
                dst_ref=R.at[(place - owner + PLANE) % PLANE],
                send_sem=gs.at[k],
                recv_sem=gr,
                device_id=plane_device(owner),
                device_id_type=MESH,
            ).start()
            return carry

        @pl.when(core == k)
        def _():
            R[0] = src[tile]

        @pl.when(core != k)
        def _():
            send(0, 0)

        lax.fori_loop(1, 16, send, 0)

        def sent():
            for count, mine in ((15, core == k), (16, core != k)):
                @pl.when(mine)
                def _():
                    pltpu.make_async_remote_copy(
                        src_ref=src.at[pl.ds(0, count)], dst_ref=R.at[pl.ds(0, count)],
                        send_sem=gs.at[k], recv_sem=gr, device_id=plane_device(place),
                        device_id_type=MESH,
                    ).wait_send()

        def parts():
            @pl.when(core == k)
            def _():
                pltpu.make_async_remote_copy(
                    src_ref=R.at[pl.ds(1, PLANE - 1)], dst_ref=R.at[pl.ds(1, PLANE - 1)],
                    send_sem=gs.at[k], recv_sem=gr, device_id=plane_device(place),
                    device_id_type=MESH,
                ).wait_recv()

        owed["parts", k], owed["scatter sent", k] = parts, sent

    grad2 = weight_grad(H, 1, lambda y, z: E[y + 1, z + 1], PLANES)
    pack(grad2, P2)
    scatter(1, P2)

    turned = full2.T
    for dx in range(3):
        WB[dx * C:dx * C + C, :] = jnp.concatenate(
            [
                turned[(26 - 3 * g - 2 + dx) * C:(26 - 3 * g - 2 + dx + 1) * C, :]
                for g in range(9)
            ],
            1,
        ).astype(bf16)

    def back(groups):
        for cells in groups:
            for (y, z), b in conv(WB, E, 1, cells, True):
                E1[y, z] = jnp.where(A1[y, z] > 0, b, 0.0).astype(bf16)

    def own_error(y, z):
        return E1[y, z]

    back(INNER)
    G[...] = weight_grad(X, 2, own_error, [sum(INNER, ())])
    settle(("halo", 1))
    rim = LOW + HIGH + SIDES
    back(rim)
    grad1 = G[...] + weight_grad(X, 2, own_error, [sum(rim[:5], ()), sum(rim[5:], ())])
    pack(grad1, P1)
    scatter(0, P1)

    for y in range(TY):
        pred_ref[:, y] = PS[y].reshape(C, TZ, XL).astype(bf16)

    settle(("parts", 1))
    settle(("parts", 0))
    own = R[0].astype(f32)
    for n in range(1, PLANE):
        own = own + R[n].astype(f32)
    Z[fs] = own.reshape(NF, 8, 128)

    def along(n, owner):
        return pltpu.make_async_remote_copy(
            src_ref=Z.at[owner], dst_ref=Z.at[owner], send_sem=zs.at[n - 1],
            recv_sem=zr.at[n - 1], device_id=(gy, gz, (fs + n) % NF), device_id_type=MESH,
        )

    def sums():
        for n in range(1, NF):
            along(n, (fs - n + NF) % NF).wait_recv()

    def sums_sent():
        for n in range(1, NF):
            along(n, fs).wait_send()

    for n in range(1, NF):
        along(n, fs).start()
    owed["sums"], owed["sums sent"] = sums, sums_sent
    settle("sums")
    total = Z[0] + Z[1] + Z[2] + Z[3]
    TT[...] = total
    squares = jnp.sum(jnp.sum(total * total, 0), 0, keepdims=True)
    rounded = squares.astype(bf16).astype(f32)
    Q[...] = jnp.concatenate(
        [TT[fs], rounded, squares - rounded, jnp.zeros((6, 128), f32)], 0
    ).astype(bf16)

    slot = core * 16 + tile
    A[slot] = Q[...]

    def spread(n, carry):
        pltpu.make_async_remote_copy(
            src_ref=Q, dst_ref=A.at[slot], send_sem=qs, recv_sem=qr,
            device_id=plane_device((place + n) % PLANE), device_id_type=MESH,
        ).start()
        return carry

    lax.fori_loop(1, PLANE, spread, 0)
    gather = pltpu.make_async_remote_copy(
        src_ref=A.at[pl.ds(0, PLANE - 1)], dst_ref=A.at[pl.ds(0, PLANE - 1)],
        send_sem=qs, recv_sem=qr, device_id=plane_device(place), device_id_type=MESH,
    )
    owed["gather"], owed["gather sent"] = gather.wait_recv, gather.wait_send
    settle("gather")

    tiles = [A[n].astype(f32) for n in range(PLANE)]
    squares = tiles[0][8:]
    for tile_in in tiles[1:]:
        squares = squares + tile_in[8:]
    norm = jnp.sqrt(jnp.sum(squares, keepdims=True))
    factor = jnp.minimum(1.0, 1.0 / (norm + 1e-06))
    for n in range(4, 8):
        settle(("load", n))
    for k, (m_ref, s_ref, u_ref) in enumerate(
        ((m1_ref, s1_ref, u1_ref), (m2_ref, s2_ref, u2_ref))
    ):
        flat = jnp.concatenate(
            [
                jnp.concatenate([tiles[k * 16 + r * 8 + t][:8] for t in range(8)], 1)
                for r in range(2)
            ],
            0,
        )
        for third in range(3):
            at = pl.ds(16 * third, 16)
            grad = factor * flat[:, COLS * third:COLS * (third + 1)]
            first = 0.9 * m_ref[at, :] + 0.1 * grad
            second = 0.999 * s_ref[at, :] + 0.001 * grad * grad
            u_ref[at, :] = first / first_bias / (jnp.sqrt(second / second_bias) + 1e-08)

    finish()


def hand_on(*refs):
    copies = [
        pltpu.make_async_copy(refs[n], refs[3 + n], refs[6].at[n]) for n in range(3)
    ]
    for copy in copies:
        copy.start()
    for copy in copies:
        copy.wait()


def shards(
    coarse_field, fine_target, kernel_one, kernel_two,
    moment_one, moment_two, second_one, second_two,
):
    hbm = pl.BlockSpec(memory_space=pltpu.HBM)
    vmem = pl.BlockSpec(memory_space=pltpu.VMEM)
    dma = pltpu.SemaphoreType.DMA
    padded = [pltpu.VMEM((TY + 2 * w, TZ + 2 * w, C, XL), bf16) for w in (2, 1, 1)]
    results = [
        jax.ShapeDtypeStruct((C, TY, TZ, XL), bf16),
        jax.ShapeDtypeStruct((C, COLS), f32),
        jax.ShapeDtypeStruct((C, COLS), f32),
    ]
    computed = pl.pallas_call(
        kernel,
        out_shape=[pltpu.VMEM(r.shape, r.dtype) for r in results],
        in_specs=[hbm] * 8,
        out_specs=[vmem] * 3,
        scratch_shapes=[
            pltpu.VMEM((C, TY, TZ, XL), bf16), pltpu.VMEM((C, TY, TZ, XL), bf16),
        ] + [pltpu.VMEM((C, COLS), f32)] * 6 + [
            dma((8,)),
            *padded,
            pltpu.VMEM((TY, TZ, C, XL), bf16),
            pltpu.VMEM((TY, TZ, C, XL), f32),
            pltpu.VMEM((TY, TZ, C, XL), f32),
            pltpu.VMEM((TY, C * TZ, XL), f32),
            pltpu.VMEM((TY, C * TZ, XL), f32),
            pltpu.VMEM((2, NF, C, 384), bf16),
            pltpu.VMEM((C3, K9), bf16),
            pltpu.VMEM((C3, K9), bf16),
            pltpu.VMEM((C3, K9), bf16),
            pltpu.VMEM((K9, C3), f32),
            pltpu.VMEM((16, NF * 8, 128), bf16),
            pltpu.VMEM((16, NF * 8, 128), bf16),
            pltpu.VMEM((PLANE, NF * 8, 128), bf16),
            pltpu.VMEM((NF, NF, 8, 128), f32),
            pltpu.VMEM((NF, 8, 128), f32),
            pltpu.VMEM((16, 128), bf16),
            pltpu.VMEM((PLANE, 16, 128), bf16),
            dma((2, 8)), dma((2, 8)),
            dma((2, 3)), dma((2, 3)),
            dma((2,)), dma,
            dma((3,)), dma((3,)),
            dma, dma,
        ],
        compiler_params=pltpu.CompilerParams(
            collective_id=0, has_side_effects=True, vmem_limit_bytes=60 << 20
        ),
    )(
        coarse_field[0], fine_target[0], kernel_one, kernel_two,
        moment_one, moment_two, second_one, second_two,
    )
    prediction, update_one, update_two = pl.pallas_call(
        hand_on,
        out_shape=results,
        in_specs=[vmem] * 3,
        out_specs=[hbm] * 3,
        scratch_shapes=[dma((3,))],
        compiler_params=pltpu.CompilerParams(vmem_limit_bytes=4 << 20),
    )(*computed)
    return prediction[None], update_one, update_two


def solution(mesh):
    field = P("fsdp", None, "gy", "gz", None)
    state = P(None, "fsdp")
    return jax.shard_map(
        shards,
        mesh=mesh,
        in_specs=(field, field) + (state,) * 6,
        out_specs=(field, state, state),
        check_vma=False,
    )
```

```python
import jax
import jax.numpy as jnp
from jax import lax
from jax.experimental import pallas as pl
from jax.experimental.pallas import tpu as pltpu
from jax.sharding import PartitionSpec as P

first_bias = 0.9999734386011124
second_bias = 0.09520785288629038

C = 48
TY, TZ, XL = 4, 8, 128
GY, GZ, NF = 4, 8, 4
PLANE = GY * GZ
TAPS = 27 * C
COLS = TAPS // NF
K9 = 9 * C
C3 = 3 * C
MESH = pl.DeviceIdType.MESH
f32, bf16 = jnp.float32, jnp.bfloat16
DIRS = [(-1, -1), (-1, 1), (-1, 0), (1, -1), (1, 1), (1, 0), (0, -1), (0, 1)]


def edge(step, size, width, sending):
    if step == 0:
        return pl.ds(width, size)
    if sending:
        return pl.ds(width if step < 0 else size, width)
    return pl.ds(size + width if step < 0 else 0, width)


def inside(value, count):
    return jnp.logical_and(value >= 0, value < count)


def roll_right(v, lane):
    return jnp.where(lane > 0, pltpu.roll(v, 1, 1), 0.0)


def roll_left(v, lane):
    return jnp.where(lane < XL - 1, pltpu.roll(v, XL - 1, 1), 0.0)


def rows9(buf, width, cells):
    off = width - 1
    return jnp.concatenate(
        [
            jnp.concatenate(
                [buf[y + dy + off, z + off:z + off + 3].reshape(C3, XL) for y, z in cells], 1
            )
            for dy in range(3)
        ],
        0,
    )


DOWN, UP, ACROSS = (0, 1, 2), (3, 4, 5), (6, 7)
CORNERS = (0, 1, 3, 4)
LOW = [((0, z), (0, z + 1)) for z in range(0, TZ, 2)]
HIGH = [((TY - 1, z), (TY - 1, z + 1)) for z in range(0, TZ, 2)]
SIDES = [((y, 0), (y, TZ - 1)) for y in range(1, TY - 1)]
INNER = [((y, z), (y, z + 1)) for y in range(1, TY - 1) for z in range(1, TZ - 1, 2)]
WIDE = [((y, z), (y, z + 1)) for y in (-1, 0, TY - 1, TY) for z in range(-1, TZ + 1, 2)]
WIDE_Z = [((y, z), (y, z + 1)) for y in range(1, TY - 1) for z in (-1, TZ - 1)]
PLANES = [tuple((y, z) for z in range(TZ)) for y in range(TY)]


def kernel(
    x_hbm, t_hbm, k1_hbm, k2_hbm, m1_hbm, m2_hbm, s1_hbm, s2_hbm,
    pred_ref, u1_ref, u2_ref,
    x_ref, t_ref, k1_ref, k2_ref, m1_ref, m2_ref, s1_ref, s2_ref, ls, X, H, E, E1, A1, TG, TS, PS, WG, W1, W2, WB, G, P1, P2, R, Z, TT, Q, A,
    hs, hr, ws, wr, gs, gr, zs, zr, qs, qr,
):
    gy = lax.axis_index("gy")
    gz = lax.axis_index("gz")
    fs = lax.axis_index("fsdp")
    core = gy % 2
    half = gy // 2
    tile = half * GZ + gz
    lane = lax.broadcasted_iota(jnp.int32, (C, XL), 1)

    loads = [
        pltpu.make_async_copy(source, ref, ls.at[n])
        for n, (source, ref) in enumerate((
            (k1_hbm, k1_ref), (x_hbm, x_ref), (k2_hbm, k2_ref), (t_hbm, t_ref),
            (m1_hbm, m1_ref), (s1_hbm, s1_ref), (m2_hbm, m2_ref), (s2_hbm, s2_ref),
        ))
    ]
    owed = {}

    def settle(name):
        owed.pop(name)()

    def finish():
        for name in list(owed):
            settle(name)

    for n, load in enumerate(loads):
        load.start()
        owed["load", n] = load.wait
    barrier = pltpu.get_barrier_semaphore()

    def further(at, size):
        out = [at]
        for _ in range(1, size):
            out.append(jnp.where(out[-1] == size - 1, 0, out[-1] + 1))
        return out

    ys, zs_at, fs_at = further(gy, GY), further(gz, GZ), further(fs, NF)
    others = [(a, b) for b in range(GZ) for a in range(GY)][1:]

    for a, b in others:
        pl.semaphore_signal(
            barrier, inc=1, device_id=(ys[a], zs_at[b], fs), device_id_type=MESH
        )
    for n in range(1, NF):
        pl.semaphore_signal(
            barrier, inc=1, device_id=(gy, gz, fs_at[n]), device_id_type=MESH
        )

    for k, ref in enumerate((k1_ref, k2_ref)):
        settle(("load", 2 * k))
        WG[k, fs] = jnp.zeros((C, 384), bf16)
        WG[k, fs, :, 0:COLS] = ref[...].astype(bf16)
    settle(("load", 1))
    for y in range(TY):
        TS[y] = x_ref[:, y].astype(f32).reshape(C * TZ, XL)
        for z in range(TZ):
            X[y + 2, z + 2] = TS[y, pl.ds(z, C, stride=TZ), :].astype(bf16)

    send_ok = [
        jnp.logical_and(inside(gy + dy, GY), inside(gz + dz, GZ)) for dy, dz in DIRS
    ]
    recv_ok = [
        jnp.logical_and(inside(gy - dy, GY), inside(gz - dz, GZ)) for dy, dz in DIRS
    ]

    def clear_outside(buf, width):
        for d, (dy, dz) in enumerate(DIRS):
            @pl.when(jnp.logical_not(recv_ok[d]))
            def _():
                region = buf.at[edge(dy, TY, width, False), edge(dz, TZ, width, False)]
                region[...] = jnp.zeros(region.shape, bf16)

    clear_outside(X, 2)
    clear_outside(E, 1)

    def halo(buf, width, phase, d, relay=False):
        dy, dz = DIRS[d]
        return pltpu.make_async_remote_copy(
            src_ref=buf.at[edge(dy, TY, width, True), edge(dz, TZ, width, not relay)],
            dst_ref=buf.at[edge(dy, TY, width, False), edge(dz, TZ, width, False)],
            send_sem=hs.at[phase, d],
            recv_sem=hr.at[phase, d],
            device_id=(
                jnp.clip(gy + dy, 0, GY - 1),
                gz if relay else jnp.clip(gz + dz, 0, GZ - 1),
                fs,
            ),
            device_id_type=MESH,
        )

    def halo_start(buf, width, phase, dirs, relay=False):
        def owe(d):
            def arrived():
                @pl.when(recv_ok[d])
                def _():
                    halo(buf, width, phase, d).wait_recv()

            def sent():
                @pl.when(send_ok[d])
                def _():
                    halo(buf, width, phase, d).wait_send()

            owed["halo", phase, d], owed["halo sent", phase, d] = arrived, sent

        for d in dirs:
            direct = send_ok[d]
            if relay and d in CORNERS:
                direct = jnp.logical_and(direct, core == (0 if DIRS[d][0] < 0 else 1))

            @pl.when(direct)
            def _():
                halo(buf, width, phase, d).start()
            owe(d)

    def relay_start(buf, width, phase):
        for d in CORNERS:
            dy, dz = DIRS[d]
            passing = jnp.logical_and(inside(gz - dz, GZ), core == (1 if dy < 0 else 0))

            @pl.when(passing)
            def _():
                halo(buf, width, phase, d, True).start()

            def sent(d=d, dy=dy, passing=passing):
                direct = jnp.logical_and(send_ok[d], core == (0 if dy < 0 else 1))

                @pl.when(jnp.logical_or(direct, passing))
                def _():
                    halo(buf, width, phase, d).wait_send()

            owed["halo sent", phase, d] = sent

    def halo_settle(phase, dirs):
        for d in dirs:
            settle(("halo", phase, d))

    def weight(k, n, owner):
        return pltpu.make_async_remote_copy(
            src_ref=WG.at[k, owner],
            dst_ref=WG.at[k, owner],
            send_sem=ws.at[k, n - 1],
            recv_sem=wr.at[k, n - 1],
            device_id=(gy, gz, fs_at[n]),
            device_id_type=MESH,
        )

    def weight_start(k):
        def arrived():
            for n in range(1, NF):
                weight(k, n, fs_at[NF - n]).wait_recv()

        def sent():
            for n in range(1, NF):
                weight(k, n, fs).wait_send()

        for n in range(1, NF):
            weight(k, n, fs).start()
        owed["weight", k], owed["weight sent", k] = arrived, sent

    pl.semaphore_wait(barrier, PLANE - 1 + NF - 1)

    weight_start(0)
    halo_start(X, 2, 0, range(8), True)
    weight_start(1)

    settle(("load", 3))
    for y in range(TY):
        TS[y] = t_ref[:, y].astype(f32).reshape(C * TZ, XL)
        for z in range(TZ):
            TG[y, z] = TS[y, pl.ds(z, C, stride=TZ), :]

    def gathered(k):
        return jnp.concatenate([WG[k, f].astype(f32)[:, :COLS] for f in range(NF)], 1)

    def forward_matrix(full, out):
        for dx in range(3):
            out[dx * C:dx * C + C, :] = jnp.concatenate(
                [full[:, (3 * g + dx) * C:(3 * g + dx + 1) * C] for g in range(9)], 1
            ).astype(bf16)

    settle(("weight", 0))
    forward_matrix(gathered(0), W1)

    def conv(w, buf, width, cells, back=False):
        out = jnp.dot(w[...], rows9(buf, width, cells), preferred_element_type=f32)
        res = []
        for h in range(len(cells)):
            q = out[:, h * XL:(h + 1) * XL]
            low, mid, high = q[:C], q[C:2 * C], q[2 * C:]
            if back:
                low, high = high, low
            res.append(mid + roll_right(low, lane) + roll_left(high, lane))
        return zip(cells, res)

    def conv1(groups):
        for cells in groups:
            for (y, z), a1 in conv(W1, X, 2, cells):
                if 0 <= y < TY and 0 <= z < TZ:
                    A1[y, z] = a1
                H[y + 1, z + 1] = jnp.maximum(a1, 0.0).astype(bf16)

    conv1(INNER)
    halo_settle(0, ACROSS)
    relay_start(X, 2, 0)
    settle(("weight", 1))
    full2 = gathered(1)
    forward_matrix(full2, W2)
    conv1(WIDE_Z)
    halo_settle(0, DOWN + UP)
    conv1(WIDE)
    clear_outside(H, 1)

    def conv2(groups):
        for cells in groups:
            for (y, z), a2 in conv(W2, H, 1, cells):
                total = X[y + 2, z + 2].astype(f32) + a2
                PS[y, pl.ds(z, C, stride=TZ), :] = total
                E[y + 1, z + 1] = (total - TG[y, z]).astype(bf16)

    conv2(LOW)
    halo_start(E, 1, 1, DOWN)
    conv2(HIGH)
    halo_start(E, 1, 1, UP)
    conv2(SIDES)
    halo_start(E, 1, 1, ACROSS)
    conv2(INNER)

    def shifted(e):
        v = e.astype(f32)
        return jnp.concatenate(
            [roll_left(v, lane).astype(bf16), e, roll_right(v, lane).astype(bf16)], 0
        )

    def weight_grad(buf, width, err, groups):
        grad = None
        for cells in groups:
            right = jnp.concatenate([shifted(err(y, z)) for y, z in cells], 1)
            part = lax.dot_general(
                rows9(buf, width, cells), right, (((1,), (1,)), ((), ())),
                preferred_element_type=f32,
            )
            grad = part if grad is None else grad + part
        return grad

    def pack(grad, out):
        grad = grad.T
        shares = []
        for f in range(NF):
            pieces = []
            for third in range(3):
                col = COLS * f
                while col < COLS * (f + 1):
                    block, i = col // C, col % C
                    width = min(C - i, COLS * (f + 1) - col)
                    g, dx = block // 3, block % 3
                    pieces.append(
                        grad[dx * C + 16 * third:dx * C + 16 * third + 16,
                             g * C + i:g * C + i + width]
                    )
                    col += width
            pieces.append(jnp.zeros((16, 1024 - 3 * COLS), f32))
            flat = jnp.concatenate(pieces, 1)
            shares.append(flat)
        for t in range(16):
            at = (slice((t // 8) * 8, (t // 8) * 8 + 8), slice((t % 8) * 128, (t % 8 + 1) * 128))
            out[t] = jnp.concatenate([flat[at] for flat in shares], 0).astype(bf16)

    def scatter(k, src):
        def send(a, b):
            to = (half if a == 0 else 1 - half) * GZ + zs_at[b]
            pltpu.make_async_remote_copy(
                src_ref=src.at[to],
                dst_ref=R.at[16 * a + 2 * b + jnp.where(core == k, 0, 1)],
                send_sem=gs.at[k],
                recv_sem=gr,
                device_id=(2 * (half if a == 0 else 1 - half) + k, zs_at[b], fs),
                device_id_type=MESH,
            ).start()

        @pl.when(core == k)
        def _():
            R[0] = src[tile]

        @pl.when(core != k)
        def _():
            send(0, 0)

        for b in range(GZ):
            for a in range(2):
                if a or b:
                    send(a, b)

        def sent():
            for count, mine in ((15, core == k), (16, core != k)):
                @pl.when(mine)
                def _():
                    pltpu.make_async_remote_copy(
                        src_ref=src.at[pl.ds(0, count)], dst_ref=R.at[pl.ds(0, count)],
                        send_sem=gs.at[k], recv_sem=gr, device_id=(gy, gz, fs),
                        device_id_type=MESH,
                    ).wait_send()

        def parts():
            @pl.when(core == k)
            def _():
                pltpu.make_async_remote_copy(
                    src_ref=R.at[pl.ds(1, PLANE - 1)], dst_ref=R.at[pl.ds(1, PLANE - 1)],
                    send_sem=gs.at[k], recv_sem=gr, device_id=(gy, gz, fs),
                    device_id_type=MESH,
                ).wait_recv()

        owed["parts", k], owed["scatter sent", k] = parts, sent

    grad2 = weight_grad(H, 1, lambda y, z: E[y + 1, z + 1], PLANES)
    pack(grad2, P2)
    scatter(1, P2)

    turned = full2.T
    for dx in range(3):
        WB[dx * C:dx * C + C, :] = jnp.concatenate(
            [
                turned[(26 - 3 * g - 2 + dx) * C:(26 - 3 * g - 2 + dx + 1) * C, :]
                for g in range(9)
            ],
            1,
        ).astype(bf16)

    def back(groups):
        for cells in groups:
            for (y, z), b in conv(WB, E, 1, cells, True):
                E1[y, z] = jnp.where(A1[y, z] > 0, b, 0.0).astype(bf16)

    def own_error(y, z):
        return E1[y, z]

    back(INNER)
    G[...] = weight_grad(X, 2, own_error, [sum(INNER, ())])
    halo_settle(1, DOWN + UP + ACROSS)
    rim = LOW + HIGH + SIDES
    back(rim)
    grad1 = G[...] + weight_grad(X, 2, own_error, [sum(rim[:5], ()), sum(rim[5:], ())])
    pack(grad1, P1)
    scatter(0, P1)

    for y in range(TY):
        pred_ref[:, y] = PS[y].reshape(C, TZ, XL).astype(bf16)

    settle(("parts", 1))
    settle(("parts", 0))
    own = R[0].astype(f32)
    for n in range(1, PLANE):
        own = own + R[n].astype(f32)
    Z[fs] = own.reshape(NF, 8, 128)

    def along(n, owner):
        return pltpu.make_async_remote_copy(
            src_ref=Z.at[owner], dst_ref=Z.at[owner], send_sem=zs.at[n - 1],
            recv_sem=zr.at[n - 1], device_id=(gy, gz, fs_at[n]), device_id_type=MESH,
        )

    def sums():
        for n in range(1, NF):
            along(n, fs_at[NF - n]).wait_recv()

    def sums_sent():
        for n in range(1, NF):
            along(n, fs).wait_send()

    for n in range(1, NF):
        along(n, fs).start()
    owed["sums"], owed["sums sent"] = sums, sums_sent
    settle("sums")
    total = Z[0] + Z[1] + Z[2] + Z[3]
    TT[...] = total
    squares = jnp.sum(jnp.sum(total * total, 0), 0, keepdims=True)
    rounded = squares.astype(bf16).astype(f32)
    Q[...] = jnp.concatenate(
        [TT[fs], rounded, squares - rounded, jnp.zeros((6, 128), f32)], 0
    ).astype(bf16)

    slot = core * 16 + tile
    A[slot] = Q[...]

    for a, b in others:
        pltpu.make_async_remote_copy(
            src_ref=Q, dst_ref=A.at[slot], send_sem=qs, recv_sem=qr,
            device_id=(ys[a], zs_at[b], fs), device_id_type=MESH,
        ).start()
    gather = pltpu.make_async_remote_copy(
        src_ref=A.at[pl.ds(0, PLANE - 1)], dst_ref=A.at[pl.ds(0, PLANE - 1)],
        send_sem=qs, recv_sem=qr, device_id=(gy, gz, fs), device_id_type=MESH,
    )
    owed["gather"], owed["gather sent"] = gather.wait_recv, gather.wait_send
    for name in list(owed):
        if name not in ("gather", "gather sent"):
            settle(name)
    settle("gather")

    tiles = [A[n].astype(f32) for n in range(PLANE)]
    squares = tiles[0][8:]
    for tile_in in tiles[1:]:
        squares = squares + tile_in[8:]
    norm = jnp.sqrt(jnp.sum(squares, keepdims=True))
    factor = jnp.minimum(1.0, 1.0 / (norm + 1e-06))
    for k, (m_ref, s_ref, u_ref) in enumerate(
        ((m1_ref, s1_ref, u1_ref), (m2_ref, s2_ref, u2_ref))
    ):
        flat = jnp.concatenate(
            [
                jnp.concatenate([tiles[k * 16 + r * 8 + t][:8] for t in range(8)], 1)
                for r in range(2)
            ],
            0,
        )
        for third in range(3):
            at = pl.ds(16 * third, 16)
            grad = factor * flat[:, COLS * third:COLS * (third + 1)]
            first = 0.9 * m_ref[at, :] + 0.1 * grad
            second = 0.999 * s_ref[at, :] + 0.001 * grad * grad
            u_ref[at, :] = first / first_bias / (jnp.sqrt(second / second_bias) + 1e-08)

    finish()


def hand_on(*refs):
    copies = [
        pltpu.make_async_copy(refs[n], refs[3 + n], refs[6].at[n]) for n in range(3)
    ]
    for copy in copies:
        copy.start()
    for copy in copies:
        copy.wait()


def shards(
    coarse_field, fine_target, kernel_one, kernel_two,
    moment_one, moment_two, second_one, second_two,
):
    hbm = pl.BlockSpec(memory_space=pltpu.HBM)
    vmem = pl.BlockSpec(memory_space=pltpu.VMEM)
    dma = pltpu.SemaphoreType.DMA
    padded = [pltpu.VMEM((TY + 2 * w, TZ + 2 * w, C, XL), bf16) for w in (2, 1, 1)]
    results = [
        jax.ShapeDtypeStruct((C, TY, TZ, XL), bf16),
        jax.ShapeDtypeStruct((C, COLS), f32),
        jax.ShapeDtypeStruct((C, COLS), f32),
    ]
    computed = pl.pallas_call(
        kernel,
        out_shape=[pltpu.VMEM(r.shape, r.dtype) for r in results],
        in_specs=[hbm] * 8,
        out_specs=[vmem] * 3,
        scratch_shapes=[
            pltpu.VMEM((C, TY, TZ, XL), bf16), pltpu.VMEM((C, TY, TZ, XL), bf16),
        ] + [pltpu.VMEM((C, COLS), f32)] * 6 + [
            dma((8,)),
            *padded,
            pltpu.VMEM((TY, TZ, C, XL), bf16),
            pltpu.VMEM((TY, TZ, C, XL), f32),
            pltpu.VMEM((TY, TZ, C, XL), f32),
            pltpu.VMEM((TY, C * TZ, XL), f32),
            pltpu.VMEM((TY, C * TZ, XL), f32),
            pltpu.VMEM((2, NF, C, 384), bf16),
            pltpu.VMEM((C3, K9), bf16),
            pltpu.VMEM((C3, K9), bf16),
            pltpu.VMEM((C3, K9), bf16),
            pltpu.VMEM((K9, C3), f32),
            pltpu.VMEM((16, NF * 8, 128), bf16),
            pltpu.VMEM((16, NF * 8, 128), bf16),
            pltpu.VMEM((PLANE, NF * 8, 128), bf16),
            pltpu.VMEM((NF, NF, 8, 128), f32),
            pltpu.VMEM((NF, 8, 128), f32),
            pltpu.VMEM((16, 128), bf16),
            pltpu.VMEM((PLANE, 16, 128), bf16),
            dma((2, 8)), dma((2, 8)),
            dma((2, 3)), dma((2, 3)),
            dma((2,)), dma,
            dma((3,)), dma((3,)),
            dma, dma,
        ],
        compiler_params=pltpu.CompilerParams(
            collective_id=0, has_side_effects=True, vmem_limit_bytes=60 << 20
        ),
    )(
        coarse_field[0], fine_target[0], kernel_one, kernel_two,
        moment_one, moment_two, second_one, second_two,
    )
    prediction, update_one, update_two = pl.pallas_call(
        hand_on,
        out_shape=results,
        in_specs=[vmem] * 3,
        out_specs=[hbm] * 3,
        scratch_shapes=[dma((3,))],
        compiler_params=pltpu.CompilerParams(vmem_limit_bytes=4 << 20),
    )(*computed)
    return prediction[None], update_one, update_two


def solution(mesh):
    field = P("fsdp", None, "gy", "gz", None)
    state = P(None, "fsdp")
    return jax.shard_map(
        shards,
        mesh=mesh,
        in_specs=(field, field) + (state,) * 6,
        out_specs=(field, state, state),
        check_vma=False,
    )
```

```python
import jax
import jax.numpy as jnp
from jax import lax
from jax.experimental import pallas as pl
from jax.experimental.pallas import tpu as pltpu
from jax.sharding import PartitionSpec as P

first_bias = 0.9999734386011124
second_bias = 0.09520785288629038

C = 48
TY, TZ, XL = 4, 8, 128
GY, GZ, NF = 4, 8, 4
PLANE = GY * GZ
TAPS = 27 * C
COLS = TAPS // NF
K9 = 9 * C
C3 = 3 * C
MESH = pl.DeviceIdType.MESH
f32, bf16 = jnp.float32, jnp.bfloat16
DIRS = [(-1, -1), (-1, 1), (-1, 0), (1, -1), (1, 1), (1, 0), (0, -1), (0, 1)]


def edge(step, size, width, sending):
    if step == 0:
        return pl.ds(width, size)
    if sending:
        return pl.ds(width if step < 0 else size, width)
    return pl.ds(size + width if step < 0 else 0, width)


def inside(value, count):
    return jnp.logical_and(value >= 0, value < count)


def roll_right(v, lane):
    return jnp.where(lane > 0, pltpu.roll(v, 1, 1), 0.0)


def roll_left(v, lane):
    return jnp.where(lane < XL - 1, pltpu.roll(v, XL - 1, 1), 0.0)


def rows9(buf, width, cells):
    off = width - 1
    return jnp.concatenate(
        [
            jnp.concatenate(
                [buf[y + dy + off, z + off:z + off + 3].reshape(C3, XL) for y, z in cells], 1
            )
            for dy in range(3)
        ],
        0,
    )


DOWN, UP, ACROSS = (0, 1, 2), (3, 4, 5), (6, 7)
CORNERS = (0, 1, 3, 4)
LOW = [((0, z), (0, z + 1)) for z in range(0, TZ, 2)]
HIGH = [((TY - 1, z), (TY - 1, z + 1)) for z in range(0, TZ, 2)]
SIDES = [((y, 0), (y, TZ - 1)) for y in range(1, TY - 1)]
INNER = [((y, z), (y, z + 1)) for y in range(1, TY - 1) for z in range(1, TZ - 1, 2)]
WIDE = [((y, z), (y, z + 1)) for y in (-1, 0, TY - 1, TY) for z in range(-1, TZ + 1, 2)]
WIDE_Z = [((y, z), (y, z + 1)) for y in range(1, TY - 1) for z in (-1, TZ - 1)]
PLANES = [tuple((y, z) for z in range(TZ)) for y in range(TY)]


def kernel(
    x_hbm, t_hbm, k1_hbm, k2_hbm, m1_hbm, m2_hbm, s1_hbm, s2_hbm,
    pred_ref, u1_ref, u2_ref,
    x_ref, t_ref, k1_ref, k2_ref, m1_ref, m2_ref, s1_ref, s2_ref, ls, X, H, E, E1, A1, TG, TS, PS, WG, W1, W2, WB, G, P1, P2, R, Z, TT, Q, A,
    hs, hr, ws, wr, gs, gr, zs, zr, qs, qr,
):
    gy = lax.axis_index("gy")
    gz = lax.axis_index("gz")
    fs = lax.axis_index("fsdp")
    core = gy % 2
    half = gy // 2
    tile = half * GZ + gz
    lane = lax.broadcasted_iota(jnp.int32, (C, XL), 1)

    loads = [
        pltpu.make_async_copy(source, ref, ls.at[n])
        for n, (source, ref) in enumerate((
            (k1_hbm, k1_ref), (x_hbm, x_ref), (k2_hbm, k2_ref), (t_hbm, t_ref),
            (m1_hbm, m1_ref), (s1_hbm, s1_ref), (m2_hbm, m2_ref), (s2_hbm, s2_ref),
        ))
    ]
    owed = {}

    def settle(name):
        owed.pop(name)()

    def finish():
        for name in list(owed):
            settle(name)

    for n, load in enumerate(loads):
        load.start()
        owed["load", n] = load.wait
    barrier = pltpu.get_barrier_semaphore()

    def further(at, size):
        out = [at]
        for _ in range(1, size):
            out.append(jnp.where(out[-1] == size - 1, 0, out[-1] + 1))
        return out

    ys, zs_at, fs_at = further(gy, GY), further(gz, GZ), further(fs, NF)
    others = [(a, b) for b in range(GZ) for a in range(GY)][1:]

    for n in range(1, NF):
        pl.semaphore_signal(
            barrier, inc=1, device_id=(gy, gz, fs_at[n]), device_id_type=MESH
        )
    for a, b in others:
        pl.semaphore_signal(
            barrier, inc=1, device_id=(ys[a], zs_at[b], fs), device_id_type=MESH
        )

    for k, ref in enumerate((k1_ref, k2_ref)):
        settle(("load", 2 * k))
        WG[k, fs] = jnp.zeros((C, 384), bf16)
        WG[k, fs, :, 0:COLS] = ref[...].astype(bf16)
    settle(("load", 1))
    for y in range(TY):
        TS[y] = x_ref[:, y].astype(f32).reshape(C * TZ, XL)
        for z in range(TZ):
            X[y + 2, z + 2] = TS[y, pl.ds(z, C, stride=TZ), :].astype(bf16)

    send_ok = [
        jnp.logical_and(inside(gy + dy, GY), inside(gz + dz, GZ)) for dy, dz in DIRS
    ]
    recv_ok = [
        jnp.logical_and(inside(gy - dy, GY), inside(gz - dz, GZ)) for dy, dz in DIRS
    ]

    def clear_outside(buf, width):
        for d, (dy, dz) in enumerate(DIRS):
            @pl.when(jnp.logical_not(recv_ok[d]))
            def _():
                region = buf.at[edge(dy, TY, width, False), edge(dz, TZ, width, False)]
                region[...] = jnp.zeros(region.shape, bf16)

    clear_outside(X, 2)
    clear_outside(E, 1)

    def halo(buf, width, phase, d, relay=False):
        dy, dz = DIRS[d]
        return pltpu.make_async_remote_copy(
            src_ref=buf.at[edge(dy, TY, width, True), edge(dz, TZ, width, not relay)],
            dst_ref=buf.at[edge(dy, TY, width, False), edge(dz, TZ, width, False)],
            send_sem=hs.at[phase, d],
            recv_sem=hr.at[phase, d],
            device_id=(
                jnp.clip(gy + dy, 0, GY - 1),
                gz if relay else jnp.clip(gz + dz, 0, GZ - 1),
                fs,
            ),
            device_id_type=MESH,
        )

    def halo_start(buf, width, phase, dirs, relay=False):
        def owe(d):
            def arrived():
                @pl.when(recv_ok[d])
                def _():
                    halo(buf, width, phase, d).wait_recv()

            def sent():
                @pl.when(send_ok[d])
                def _():
                    halo(buf, width, phase, d).wait_send()

            owed["halo", phase, d], owed["halo sent", phase, d] = arrived, sent

        for d in dirs:
            direct = send_ok[d]
            if relay and d in CORNERS:
                direct = jnp.logical_and(direct, core == (0 if DIRS[d][0] < 0 else 1))

            @pl.when(direct)
            def _():
                halo(buf, width, phase, d).start()
            owe(d)

    def relay_start(buf, width, phase):
        for d in CORNERS:
            dy, dz = DIRS[d]
            passing = jnp.logical_and(inside(gz - dz, GZ), core == (1 if dy < 0 else 0))

            @pl.when(passing)
            def _():
                halo(buf, width, phase, d, True).start()

            def sent(d=d, dy=dy, passing=passing):
                direct = jnp.logical_and(send_ok[d], core == (0 if dy < 0 else 1))

                @pl.when(jnp.logical_or(direct, passing))
                def _():
                    halo(buf, width, phase, d).wait_send()

            owed["halo sent", phase, d] = sent

    def halo_settle(phase, dirs):
        for d in dirs:
            settle(("halo", phase, d))

    def weight(k, n, owner):
        return pltpu.make_async_remote_copy(
            src_ref=WG.at[k, owner],
            dst_ref=WG.at[k, owner],
            send_sem=ws.at[k, n - 1],
            recv_sem=wr.at[k, n - 1],
            device_id=(gy, gz, fs_at[n]),
            device_id_type=MESH,
        )

    def weight_start(k):
        def arrived():
            for n in range(1, NF):
                weight(k, n, fs_at[NF - n]).wait_recv()

        def sent():
            for n in range(1, NF):
                weight(k, n, fs).wait_send()

        for n in range(1, NF):
            weight(k, n, fs).start()
        owed["weight", k], owed["weight sent", k] = arrived, sent

    pl.semaphore_wait(barrier, PLANE - 1 + NF - 1)

    weight_start(0)
    halo_start(X, 2, 0, range(8), True)
    weight_start(1)

    settle(("load", 3))
    for y in range(TY):
        TS[y] = t_ref[:, y].astype(f32).reshape(C * TZ, XL)
        for z in range(TZ):
            TG[y, z] = TS[y, pl.ds(z, C, stride=TZ), :]

    def gathered(k):
        return jnp.concatenate([WG[k, f].astype(f32)[:, :COLS] for f in range(NF)], 1)

    def forward_matrix(full, out):
        for dx in range(3):
            out[dx * C:dx * C + C, :] = jnp.concatenate(
                [full[:, (3 * g + dx) * C:(3 * g + dx + 1) * C] for g in range(9)], 1
            ).astype(bf16)

    settle(("weight", 0))
    forward_matrix(gathered(0), W1)

    def conv(w, buf, width, cells, back=False):
        out = jnp.dot(w[...], rows9(buf, width, cells), preferred_element_type=f32)
        res = []
        for h in range(len(cells)):
            q = out[:, h * XL:(h + 1) * XL]
            low, mid, high = q[:C], q[C:2 * C], q[2 * C:]
            if back:
                low, high = high, low
            res.append(mid + roll_right(low, lane) + roll_left(high, lane))
        return zip(cells, res)

    def conv1(groups):
        for cells in groups:
            for (y, z), a1 in conv(W1, X, 2, cells):
                if 0 <= y < TY and 0 <= z < TZ:
                    A1[y, z] = a1
                H[y + 1, z + 1] = jnp.maximum(a1, 0.0).astype(bf16)

    conv1(INNER)
    halo_settle(0, ACROSS)
    relay_start(X, 2, 0)
    settle(("weight", 1))
    full2 = gathered(1)
    forward_matrix(full2, W2)
    conv1(WIDE_Z)
    halo_settle(0, DOWN + UP)
    conv1(WIDE)
    clear_outside(H, 1)

    def conv2(groups):
        for cells in groups:
            for (y, z), a2 in conv(W2, H, 1, cells):
                total = X[y + 2, z + 2].astype(f32) + a2
                PS[y, pl.ds(z, C, stride=TZ), :] = total
                E[y + 1, z + 1] = (total - TG[y, z]).astype(bf16)

    conv2(LOW)
    halo_start(E, 1, 1, DOWN)
    conv2(HIGH)
    halo_start(E, 1, 1, UP)
    conv2(SIDES)
    halo_start(E, 1, 1, ACROSS)
    conv2(INNER)

    def shifted(e):
        v = e.astype(f32)
        return jnp.concatenate(
            [roll_left(v, lane).astype(bf16), e, roll_right(v, lane).astype(bf16)], 0
        )

    def weight_grad(buf, width, err, groups):
        grad = None
        for cells in groups:
            right = jnp.concatenate([shifted(err(y, z)) for y, z in cells], 1)
            part = lax.dot_general(
                rows9(buf, width, cells), right, (((1,), (1,)), ((), ())),
                preferred_element_type=f32,
            )
            grad = part if grad is None else grad + part
        return grad

    def pack(grad, out):
        grad = grad.T
        shares = []
        for f in range(NF):
            pieces = []
            for third in range(3):
                col = COLS * f
                while col < COLS * (f + 1):
                    block, i = col // C, col % C
                    width = min(C - i, COLS * (f + 1) - col)
                    g, dx = block // 3, block % 3
                    pieces.append(
                        grad[dx * C + 16 * third:dx * C + 16 * third + 16,
                             g * C + i:g * C + i + width]
                    )
                    col += width
            pieces.append(jnp.zeros((16, 1024 - 3 * COLS), f32))
            flat = jnp.concatenate(pieces, 1)
            shares.append(flat)
        for t in range(16):
            at = (slice((t // 8) * 8, (t // 8) * 8 + 8), slice((t % 8) * 128, (t % 8 + 1) * 128))
            out[t] = jnp.concatenate([flat[at] for flat in shares], 0).astype(bf16)

    def scatter(k, src):
        def send(a, b):
            to = (half if a == 0 else 1 - half) * GZ + zs_at[b]
            pltpu.make_async_remote_copy(
                src_ref=src.at[to],
                dst_ref=R.at[16 * a + 2 * b + jnp.where(core == k, 0, 1)],
                send_sem=gs.at[k],
                recv_sem=gr,
                device_id=(2 * (half if a == 0 else 1 - half) + k, zs_at[b], fs),
                device_id_type=MESH,
            ).start()

        @pl.when(core == k)
        def _():
            R[0] = src[tile]

        @pl.when(core != k)
        def _():
            send(0, 0)

        for b in range(GZ):
            for a in range(2):
                if a or b:
                    send(a, b)

        def sent():
            for count, mine in ((15, core == k), (16, core != k)):
                @pl.when(mine)
                def _():
                    pltpu.make_async_remote_copy(
                        src_ref=src.at[pl.ds(0, count)], dst_ref=R.at[pl.ds(0, count)],
                        send_sem=gs.at[k], recv_sem=gr, device_id=(gy, gz, fs),
                        device_id_type=MESH,
                    ).wait_send()

        def parts():
            @pl.when(core == k)
            def _():
                pltpu.make_async_remote_copy(
                    src_ref=R.at[pl.ds(1, PLANE - 1)], dst_ref=R.at[pl.ds(1, PLANE - 1)],
                    send_sem=gs.at[k], recv_sem=gr, device_id=(gy, gz, fs),
                    device_id_type=MESH,
                ).wait_recv()

        owed["parts", k], owed["scatter sent", k] = parts, sent

    grad2 = weight_grad(H, 1, lambda y, z: E[y + 1, z + 1], PLANES)
    pack(grad2, P2)
    scatter(1, P2)

    turned = full2.T
    for dx in range(3):
        WB[dx * C:dx * C + C, :] = jnp.concatenate(
            [
                turned[(26 - 3 * g - 2 + dx) * C:(26 - 3 * g - 2 + dx + 1) * C, :]
                for g in range(9)
            ],
            1,
        ).astype(bf16)

    def back(groups):
        for cells in groups:
            for (y, z), b in conv(WB, E, 1, cells, True):
                E1[y, z] = jnp.where(A1[y, z] > 0, b, 0.0).astype(bf16)

    def own_error(y, z):
        return E1[y, z]

    back(INNER)
    G[...] = weight_grad(X, 2, own_error, [sum(INNER, ())])
    halo_settle(1, DOWN + UP + ACROSS)
    rim = LOW + HIGH + SIDES
    back(rim)
    grad1 = G[...] + weight_grad(X, 2, own_error, [sum(rim, ())])
    pack(grad1, P1)
    scatter(0, P1)

    for y in range(TY):
        pred_ref[:, y] = PS[y].reshape(C, TZ, XL).astype(bf16)

    settle(("parts", 1))
    settle(("parts", 0))
    own = R[0].astype(f32)
    for n in range(1, PLANE):
        own = own + R[n].astype(f32)
    Z[fs] = own.astype(bf16)

    def along(n, owner):
        return pltpu.make_async_remote_copy(
            src_ref=Z.at[owner], dst_ref=Z.at[owner], send_sem=zs.at[n - 1],
            recv_sem=zr.at[n - 1], device_id=(gy, gz, fs_at[n]), device_id_type=MESH,
        )

    def sums():
        for n in range(1, NF):
            along(n, fs_at[NF - n]).wait_recv()

    def sums_sent():
        for n in range(1, NF):
            along(n, fs).wait_send()

    for n in range(1, NF):
        along(n, fs).start()
    owed["sums"], owed["sums sent"] = sums, sums_sent
    settle("sums")
    total = sum(Z[n].astype(f32) for n in range(NF)).reshape(NF, 8, 128)
    TT[...] = total
    squares = jnp.sum(jnp.sum(total * total, 0), 0, keepdims=True)
    rounded = squares.astype(bf16).astype(f32)
    Q[...] = jnp.concatenate(
        [TT[fs], rounded, squares - rounded, jnp.zeros((6, 128), f32)], 0
    ).astype(bf16)

    slot = core * 16 + tile
    A[slot] = Q[...]

    for a, b in others:
        pltpu.make_async_remote_copy(
            src_ref=Q, dst_ref=A.at[slot], send_sem=qs, recv_sem=qr,
            device_id=(ys[a], zs_at[b], fs), device_id_type=MESH,
        ).start()
    gather = pltpu.make_async_remote_copy(
        src_ref=A.at[pl.ds(0, PLANE - 1)], dst_ref=A.at[pl.ds(0, PLANE - 1)],
        send_sem=qs, recv_sem=qr, device_id=(gy, gz, fs), device_id_type=MESH,
    )
    owed["gather"], owed["gather sent"] = gather.wait_recv, gather.wait_send
    for name in list(owed):
        if name not in ("gather", "gather sent"):
            settle(name)
    settle("gather")

    tiles = [A[n].astype(f32) for n in range(PLANE)]
    squares = tiles[0][8:]
    for tile_in in tiles[1:]:
        squares = squares + tile_in[8:]
    norm = jnp.sqrt(jnp.sum(squares, keepdims=True))
    factor = jnp.minimum(1.0, 1.0 / (norm + 1e-06))
    for k, (m_ref, s_ref, u_ref) in enumerate(
        ((m1_ref, s1_ref, u1_ref), (m2_ref, s2_ref, u2_ref))
    ):
        flat = jnp.concatenate(
            [
                jnp.concatenate([tiles[k * 16 + r * 8 + t][:8] for t in range(8)], 1)
                for r in range(2)
            ],
            0,
        )
        for third in range(3):
            at = pl.ds(16 * third, 16)
            grad = factor * flat[:, COLS * third:COLS * (third + 1)]
            first = 0.9 * m_ref[at, :] + 0.1 * grad
            second = 0.999 * s_ref[at, :] + 0.001 * grad * grad
            u_ref[at, :] = first / first_bias / (jnp.sqrt(second / second_bias) + 1e-08)

    finish()


def hand_on(*refs):
    copies = [
        pltpu.make_async_copy(refs[n], refs[3 + n], refs[6].at[n]) for n in range(3)
    ]
    for copy in copies:
        copy.start()
    for copy in copies:
        copy.wait()


def shards(
    coarse_field, fine_target, kernel_one, kernel_two,
    moment_one, moment_two, second_one, second_two,
):
    hbm = pl.BlockSpec(memory_space=pltpu.HBM)
    vmem = pl.BlockSpec(memory_space=pltpu.VMEM)
    dma = pltpu.SemaphoreType.DMA
    padded = [pltpu.VMEM((TY + 2 * w, TZ + 2 * w, C, XL), bf16) for w in (2, 1, 1)]
    results = [
        jax.ShapeDtypeStruct((C, TY, TZ, XL), bf16),
        jax.ShapeDtypeStruct((C, COLS), f32),
        jax.ShapeDtypeStruct((C, COLS), f32),
    ]
    computed = pl.pallas_call(
        kernel,
        out_shape=[pltpu.VMEM(r.shape, r.dtype) for r in results],
        in_specs=[hbm] * 8,
        out_specs=[vmem] * 3,
        scratch_shapes=[
            pltpu.VMEM((C, TY, TZ, XL), bf16), pltpu.VMEM((C, TY, TZ, XL), bf16),
        ] + [pltpu.VMEM((C, COLS), f32)] * 6 + [
            dma((8,)),
            *padded,
            pltpu.VMEM((TY, TZ, C, XL), bf16),
            pltpu.VMEM((TY, TZ, C, XL), f32),
            pltpu.VMEM((TY, TZ, C, XL), f32),
            pltpu.VMEM((TY, C * TZ, XL), f32),
            pltpu.VMEM((TY, C * TZ, XL), f32),
            pltpu.VMEM((2, NF, C, 384), bf16),
            pltpu.VMEM((C3, K9), bf16),
            pltpu.VMEM((C3, K9), bf16),
            pltpu.VMEM((C3, K9), bf16),
            pltpu.VMEM((K9, C3), f32),
            pltpu.VMEM((16, NF * 8, 128), bf16),
            pltpu.VMEM((16, NF * 8, 128), bf16),
            pltpu.VMEM((PLANE, NF * 8, 128), bf16),
            pltpu.VMEM((NF, NF * 8, 128), bf16),
            pltpu.VMEM((NF, 8, 128), f32),
            pltpu.VMEM((16, 128), bf16),
            pltpu.VMEM((PLANE, 16, 128), bf16),
            dma((2, 8)), dma((2, 8)),
            dma((2, 3)), dma((2, 3)),
            dma((2,)), dma,
            dma((3,)), dma((3,)),
            dma, dma,
        ],
        compiler_params=pltpu.CompilerParams(
            collective_id=0, has_side_effects=True, vmem_limit_bytes=60 << 20
        ),
    )(
        coarse_field[0], fine_target[0], kernel_one, kernel_two,
        moment_one, moment_two, second_one, second_two,
    )
    prediction, update_one, update_two = pl.pallas_call(
        hand_on,
        out_shape=results,
        in_specs=[vmem] * 3,
        out_specs=[hbm] * 3,
        scratch_shapes=[dma((3,))],
        compiler_params=pltpu.CompilerParams(vmem_limit_bytes=4 << 20),
    )(*computed)
    return prediction[None], update_one, update_two


def solution(mesh):
    field = P("fsdp", None, "gy", "gz", None)
    state = P(None, "fsdp")
    return jax.shard_map(
        shards,
        mesh=mesh,
        in_specs=(field, field) + (state,) * 6,
        out_specs=(field, state, state),
        check_vma=False,
    )
```

```python
import jax
import jax.numpy as jnp
from jax import lax
from jax.experimental import pallas as pl
from jax.experimental.pallas import tpu as pltpu
from jax.sharding import PartitionSpec as P

first_bias = 0.9999734386011124
second_bias = 0.09520785288629038

C = 48
TY, TZ, XL = 4, 8, 128
GY, GZ, NF = 4, 8, 4
PLANE = GY * GZ
TAPS = 27 * C
COLS = TAPS // NF
K9 = 9 * C
C3 = 3 * C
MESH = pl.DeviceIdType.MESH
f32, bf16 = jnp.float32, jnp.bfloat16
DIRS = [(-1, -1), (-1, 1), (-1, 0), (1, -1), (1, 1), (1, 0), (0, -1), (0, 1)]


def edge(step, size, width, sending):
    if step == 0:
        return pl.ds(width, size)
    if sending:
        return pl.ds(width if step < 0 else size, width)
    return pl.ds(size + width if step < 0 else 0, width)


def inside(value, count):
    return jnp.logical_and(value >= 0, value < count)


def roll_right(v, lane):
    return jnp.where(lane > 0, pltpu.roll(v, 1, 1), 0.0)


def roll_left(v, lane):
    return jnp.where(lane < XL - 1, pltpu.roll(v, XL - 1, 1), 0.0)


def rows9(buf, width, cells):
    off = width - 1
    return jnp.concatenate(
        [
            jnp.concatenate(
                [buf[y + dy + off, z + off:z + off + 3].reshape(C3, XL) for y, z in cells], 1
            )
            for dy in range(3)
        ],
        0,
    )


DOWN, UP, ACROSS = (0, 1, 2), (3, 4, 5), (6, 7)
CORNERS = (0, 1, 3, 4)
LOW = [((0, z), (0, z + 1)) for z in range(0, TZ, 2)]
HIGH = [((TY - 1, z), (TY - 1, z + 1)) for z in range(0, TZ, 2)]
SIDES = [((y, 0), (y, TZ - 1)) for y in range(1, TY - 1)]
INNER = [((y, z), (y, z + 1)) for y in range(1, TY - 1) for z in range(1, TZ - 1, 2)]
WIDE = [((y, z), (y, z + 1)) for y in (-1, 0, TY - 1, TY) for z in range(-1, TZ + 1, 2)]
WIDE_Z = [((y, z), (y, z + 1)) for y in range(1, TY - 1) for z in (-1, TZ - 1)]
PLANES = [tuple((y, z) for z in range(TZ)) for y in range(TY)]


def kernel(
    x_hbm, t_hbm, k1_hbm, k2_hbm, m1_hbm, m2_hbm, s1_hbm, s2_hbm,
    pred_ref, u1_ref, u2_ref,
    x_ref, t_ref, k1_ref, k2_ref, m1_ref, m2_ref, s1_ref, s2_ref, ls, X, H, E, E1, A1, TG, TS, PS, WG, W1, W2, WB, G, P1, P2, R, Z, TT, Q, A,
    hs, hr, ws, wr, gs, gr, zs, zr, qs, qr,
):
    gy = lax.axis_index("gy")
    gz = lax.axis_index("gz")
    fs = lax.axis_index("fsdp")
    core = gy % 2
    half = gy // 2
    tile = half * GZ + gz
    lane = lax.broadcasted_iota(jnp.int32, (C, XL), 1)

    loads = [
        pltpu.make_async_copy(source, ref, ls.at[n])
        for n, (source, ref) in enumerate((
            (k1_hbm, k1_ref), (x_hbm, x_ref), (k2_hbm, k2_ref), (t_hbm, t_ref),
            (m1_hbm, m1_ref), (s1_hbm, s1_ref), (m2_hbm, m2_ref), (s2_hbm, s2_ref),
        ))
    ]
    owed = {}

    def settle(name):
        owed.pop(name)()

    def finish():
        for name in list(owed):
            settle(name)

    for n, load in enumerate(loads):
        load.start()
        owed["load", n] = load.wait
    barrier = pltpu.get_barrier_semaphore()

    def further(at, size):
        out = [at]
        for _ in range(1, size):
            out.append(jnp.where(out[-1] == size - 1, 0, out[-1] + 1))
        return out

    ys, zs_at, fs_at = further(gy, GY), further(gz, GZ), further(fs, NF)
    others = [(a, b) for b in range(GZ) for a in range(GY)][1:]

    for n in range(1, NF):
        pl.semaphore_signal(
            barrier, inc=1, device_id=(gy, gz, fs_at[n]), device_id_type=MESH
        )
    for a, b in others:
        pl.semaphore_signal(
            barrier, inc=1, device_id=(ys[a], zs_at[b], fs), device_id_type=MESH
        )

    for k, ref in enumerate((k1_ref, k2_ref)):
        settle(("load", 2 * k))
        WG[k, fs] = jnp.zeros((C, 384), bf16)
        WG[k, fs, :, 0:COLS] = ref[...].astype(bf16)
    settle(("load", 1))
    for y in range(TY):
        TS[y] = x_ref[:, y].astype(f32).reshape(C * TZ, XL)
        for z in range(TZ):
            X[y + 2, z + 2] = TS[y, pl.ds(z, C, stride=TZ), :].astype(bf16)

    send_ok = [
        jnp.logical_and(inside(gy + dy, GY), inside(gz + dz, GZ)) for dy, dz in DIRS
    ]
    recv_ok = [
        jnp.logical_and(inside(gy - dy, GY), inside(gz - dz, GZ)) for dy, dz in DIRS
    ]

    def clear_outside(buf, width):
        for d, (dy, dz) in enumerate(DIRS):
            @pl.when(jnp.logical_not(recv_ok[d]))
            def _():
                region = buf.at[edge(dy, TY, width, False), edge(dz, TZ, width, False)]
                region[...] = jnp.zeros(region.shape, bf16)

    clear_outside(X, 2)
    clear_outside(E, 1)

    def halo(buf, width, phase, d, relay=False):
        dy, dz = DIRS[d]
        return pltpu.make_async_remote_copy(
            src_ref=buf.at[edge(dy, TY, width, True), edge(dz, TZ, width, not relay)],
            dst_ref=buf.at[edge(dy, TY, width, False), edge(dz, TZ, width, False)],
            send_sem=hs.at[phase, d],
            recv_sem=hr.at[phase, d],
            device_id=(
                jnp.clip(gy + dy, 0, GY - 1),
                gz if relay else jnp.clip(gz + dz, 0, GZ - 1),
                fs,
            ),
            device_id_type=MESH,
        )

    def halo_start(buf, width, phase, dirs, relay=False):
        def owe(d):
            def arrived():
                @pl.when(recv_ok[d])
                def _():
                    halo(buf, width, phase, d).wait_recv()

            def sent():
                @pl.when(send_ok[d])
                def _():
                    halo(buf, width, phase, d).wait_send()

            owed["halo", phase, d], owed["halo sent", phase, d] = arrived, sent

        for d in dirs:
            direct = send_ok[d]
            if relay and d in CORNERS:
                direct = jnp.logical_and(direct, core == (0 if DIRS[d][0] < 0 else 1))

            @pl.when(direct)
            def _():
                halo(buf, width, phase, d).start()
            owe(d)

    def relay_start(buf, width, phase):
        for d in CORNERS:
            dy, dz = DIRS[d]
            passing = jnp.logical_and(inside(gz - dz, GZ), core == (1 if dy < 0 else 0))

            @pl.when(passing)
            def _():
                halo(buf, width, phase, d, True).start()

            def sent(d=d, dy=dy, passing=passing):
                direct = jnp.logical_and(send_ok[d], core == (0 if dy < 0 else 1))

                @pl.when(jnp.logical_or(direct, passing))
                def _():
                    halo(buf, width, phase, d).wait_send()

            owed["halo sent", phase, d] = sent

    def halo_settle(phase, dirs):
        for d in dirs:
            settle(("halo", phase, d))

    def weight(k, n, owner):
        return pltpu.make_async_remote_copy(
            src_ref=WG.at[k, owner],
            dst_ref=WG.at[k, owner],
            send_sem=ws.at[k, n - 1],
            recv_sem=wr.at[k, n - 1],
            device_id=(gy, gz, fs_at[n]),
            device_id_type=MESH,
        )

    def weight_start(k):
        def arrived():
            for n in range(1, NF):
                weight(k, n, fs_at[NF - n]).wait_recv()

        def sent():
            for n in range(1, NF):
                weight(k, n, fs).wait_send()

        for n in range(1, NF):
            weight(k, n, fs).start()
        owed["weight", k], owed["weight sent", k] = arrived, sent

    pl.semaphore_wait(barrier, PLANE - 1 + NF - 1)

    weight_start(0)
    halo_start(X, 2, 0, range(8), True)
    weight_start(1)

    settle(("load", 3))
    for y in range(TY):
        TS[y] = t_ref[:, y].astype(f32).reshape(C * TZ, XL)
        for z in range(TZ):
            TG[y, z] = TS[y, pl.ds(z, C, stride=TZ), :]

    def gathered(k):
        return jnp.concatenate([WG[k, f].astype(f32)[:, :COLS] for f in range(NF)], 1)

    def forward_matrix(full, out):
        for dx in range(3):
            out[dx * C:dx * C + C, :] = jnp.concatenate(
                [full[:, (3 * g + dx) * C:(3 * g + dx + 1) * C] for g in range(9)], 1
            ).astype(bf16)

    settle(("weight", 0))
    forward_matrix(gathered(0), W1)

    def conv(w, buf, width, cells, back=False):
        out = jnp.dot(w[...], rows9(buf, width, cells), preferred_element_type=f32)
        res = []
        for h in range(len(cells)):
            q = out[:, h * XL:(h + 1) * XL]
            low, mid, high = q[:C], q[C:2 * C], q[2 * C:]
            if back:
                low, high = high, low
            res.append(mid + roll_right(low, lane) + roll_left(high, lane))
        return zip(cells, res)

    def conv1(groups):
        for cells in groups:
            for (y, z), a1 in conv(W1, X, 2, cells):
                if 0 <= y < TY and 0 <= z < TZ:
                    A1[y, z] = a1
                H[y + 1, z + 1] = jnp.maximum(a1, 0.0).astype(bf16)

    conv1(INNER)
    halo_settle(0, ACROSS)
    relay_start(X, 2, 0)
    conv1(WIDE_Z)
    halo_settle(0, DOWN + UP)
    conv1(WIDE)
    clear_outside(H, 1)
    settle(("weight", 1))
    full2 = gathered(1)
    forward_matrix(full2, W2)

    def conv2(groups):
        for cells in groups:
            for (y, z), a2 in conv(W2, H, 1, cells):
                total = X[y + 2, z + 2].astype(f32) + a2
                PS[y, pl.ds(z, C, stride=TZ), :] = total
                E[y + 1, z + 1] = (total - TG[y, z]).astype(bf16)

    conv2(LOW)
    halo_start(E, 1, 1, DOWN)
    conv2(HIGH)
    halo_start(E, 1, 1, UP)
    conv2(SIDES)
    halo_start(E, 1, 1, ACROSS)
    conv2(INNER)

    def shifted(e):
        v = e.astype(f32)
        return jnp.concatenate(
            [roll_left(v, lane).astype(bf16), e, roll_right(v, lane).astype(bf16)], 0
        )

    def weight_grad(buf, width, err, groups):
        grad = None
        for cells in groups:
            right = jnp.concatenate([shifted(err(y, z)) for y, z in cells], 1)
            part = lax.dot_general(
                rows9(buf, width, cells), right, (((1,), (1,)), ((), ())),
                preferred_element_type=f32,
            )
            grad = part if grad is None else grad + part
        return grad

    def pack(grad, out):
        grad = grad.T
        shares = []
        for f in range(NF):
            pieces = []
            for third in range(3):
                col = COLS * f
                while col < COLS * (f + 1):
                    block, i = col // C, col % C
                    width = min(C - i, COLS * (f + 1) - col)
                    g, dx = block // 3, block % 3
                    pieces.append(
                        grad[dx * C + 16 * third:dx * C + 16 * third + 16,
                             g * C + i:g * C + i + width]
                    )
                    col += width
            pieces.append(jnp.zeros((16, 1024 - 3 * COLS), f32))
            flat = jnp.concatenate(pieces, 1)
            shares.append(flat)
        for t in range(16):
            at = (slice((t // 8) * 8, (t // 8) * 8 + 8), slice((t % 8) * 128, (t % 8 + 1) * 128))
            out[t] = jnp.concatenate([flat[at] for flat in shares], 0).astype(bf16)

    def scatter(k, src):
        def send(a, b):
            to = (half if a == 0 else 1 - half) * GZ + zs_at[b]
            pltpu.make_async_remote_copy(
                src_ref=src.at[to],
                dst_ref=R.at[16 * a + 2 * b + jnp.where(core == k, 0, 1)],
                send_sem=gs.at[k],
                recv_sem=gr,
                device_id=(2 * (half if a == 0 else 1 - half) + k, zs_at[b], fs),
                device_id_type=MESH,
            ).start()

        @pl.when(core == k)
        def _():
            R[0] = src[tile]

        @pl.when(core != k)
        def _():
            send(0, 0)

        for b in range(GZ):
            for a in range(2):
                if a or b:
                    send(a, b)

        def sent():
            for count, mine in ((15, core == k), (16, core != k)):
                @pl.when(mine)
                def _():
                    pltpu.make_async_remote_copy(
                        src_ref=src.at[pl.ds(0, count)], dst_ref=R.at[pl.ds(0, count)],
                        send_sem=gs.at[k], recv_sem=gr, device_id=(gy, gz, fs),
                        device_id_type=MESH,
                    ).wait_send()

        def parts():
            @pl.when(core == k)
            def _():
                pltpu.make_async_remote_copy(
                    src_ref=R.at[pl.ds(1, PLANE - 1)], dst_ref=R.at[pl.ds(1, PLANE - 1)],
                    send_sem=gs.at[k], recv_sem=gr, device_id=(gy, gz, fs),
                    device_id_type=MESH,
                ).wait_recv()

        owed["parts", k], owed["scatter sent", k] = parts, sent

    grad2 = weight_grad(H, 1, lambda y, z: E[y + 1, z + 1], PLANES)
    pack(grad2, P2)
    scatter(1, P2)

    turned = full2.T
    for dx in range(3):
        WB[dx * C:dx * C + C, :] = jnp.concatenate(
            [
                turned[(26 - 3 * g - 2 + dx) * C:(26 - 3 * g - 2 + dx + 1) * C, :]
                for g in range(9)
            ],
            1,
        ).astype(bf16)

    def back(groups):
        for cells in groups:
            for (y, z), b in conv(WB, E, 1, cells, True):
                E1[y, z] = jnp.where(A1[y, z] > 0, b, 0.0).astype(bf16)

    def own_error(y, z):
        return E1[y, z]

    back(INNER)
    G[...] = weight_grad(X, 2, own_error, [sum(INNER, ())])
    halo_settle(1, DOWN + UP + ACROSS)
    rim = LOW + HIGH + SIDES
    back(rim)
    grad1 = G[...] + weight_grad(X, 2, own_error, [sum(rim, ())])
    pack(grad1, P1)
    scatter(0, P1)

    for y in range(TY):
        pred_ref[:, y] = PS[y].reshape(C, TZ, XL).astype(bf16)

    settle(("parts", 1))
    settle(("parts", 0))
    own = R[0].astype(f32)
    for n in range(1, PLANE):
        own = own + R[n].astype(f32)
    Z[fs] = own.astype(bf16)

    def along(n, owner):
        return pltpu.make_async_remote_copy(
            src_ref=Z.at[owner], dst_ref=Z.at[owner], send_sem=zs.at[n - 1],
            recv_sem=zr.at[n - 1], device_id=(gy, gz, fs_at[n]), device_id_type=MESH,
        )

    def sums():
        for n in range(1, NF):
            along(n, fs_at[NF - n]).wait_recv()

    def sums_sent():
        for n in range(1, NF):
            along(n, fs).wait_send()

    for n in range(1, NF):
        along(n, fs).start()
    owed["sums"], owed["sums sent"] = sums, sums_sent
    settle("sums")
    total = sum(Z[n].astype(f32) for n in range(NF)).reshape(NF, 8, 128)
    TT[...] = total
    squares = jnp.sum(jnp.sum(total * total, 0), 0, keepdims=True)
    rounded = squares.astype(bf16).astype(f32)
    Q[...] = jnp.concatenate(
        [TT[fs], rounded, squares - rounded, jnp.zeros((6, 128), f32)], 0
    ).astype(bf16)

    slot = core * 16 + tile
    A[slot] = Q[...]

    for a, b in others:
        pltpu.make_async_remote_copy(
            src_ref=Q, dst_ref=A.at[slot], send_sem=qs, recv_sem=qr,
            device_id=(ys[a], zs_at[b], fs), device_id_type=MESH,
        ).start()
    gather = pltpu.make_async_remote_copy(
        src_ref=A.at[pl.ds(0, PLANE - 1)], dst_ref=A.at[pl.ds(0, PLANE - 1)],
        send_sem=qs, recv_sem=qr, device_id=(gy, gz, fs), device_id_type=MESH,
    )
    owed["gather"], owed["gather sent"] = gather.wait_recv, gather.wait_send
    for name in list(owed):
        if name not in ("gather", "gather sent"):
            settle(name)
    settle("gather")

    tiles = [A[n].astype(f32) for n in range(PLANE)]
    squares = tiles[0][8:]
    for tile_in in tiles[1:]:
        squares = squares + tile_in[8:]
    norm = jnp.sqrt(jnp.sum(squares, keepdims=True))
    factor = jnp.minimum(1.0, 1.0 / (norm + 1e-06))
    for k, (m_ref, s_ref, u_ref) in enumerate(
        ((m1_ref, s1_ref, u1_ref), (m2_ref, s2_ref, u2_ref))
    ):
        flat = jnp.concatenate(
            [
                jnp.concatenate([tiles[k * 16 + r * 8 + t][:8] for t in range(8)], 1)
                for r in range(2)
            ],
            0,
        )
        for third in range(3):
            at = pl.ds(16 * third, 16)
            grad = factor * flat[:, COLS * third:COLS * (third + 1)]
            first = 0.9 * m_ref[at, :] + 0.1 * grad
            second = 0.999 * s_ref[at, :] + 0.001 * grad * grad
            u_ref[at, :] = first / first_bias / (jnp.sqrt(second / second_bias) + 1e-08)

    finish()


def hand_on(*refs):
    copies = [
        pltpu.make_async_copy(refs[n], refs[3 + n], refs[6].at[n]) for n in range(3)
    ]
    for copy in copies:
        copy.start()
    for copy in copies:
        copy.wait()


def shards(
    coarse_field, fine_target, kernel_one, kernel_two,
    moment_one, moment_two, second_one, second_two,
):
    hbm = pl.BlockSpec(memory_space=pltpu.HBM)
    vmem = pl.BlockSpec(memory_space=pltpu.VMEM)
    dma = pltpu.SemaphoreType.DMA
    padded = [pltpu.VMEM((TY + 2 * w, TZ + 2 * w, C, XL), bf16) for w in (2, 1, 1)]
    results = [
        jax.ShapeDtypeStruct((C, TY, TZ, XL), bf16),
        jax.ShapeDtypeStruct((C, COLS), f32),
        jax.ShapeDtypeStruct((C, COLS), f32),
    ]
    computed = pl.pallas_call(
        kernel,
        out_shape=[pltpu.VMEM(r.shape, r.dtype) for r in results],
        in_specs=[hbm] * 8,
        out_specs=[vmem] * 3,
        scratch_shapes=[
            pltpu.VMEM((C, TY, TZ, XL), bf16), pltpu.VMEM((C, TY, TZ, XL), bf16),
        ] + [pltpu.VMEM((C, COLS), f32)] * 6 + [
            dma((8,)),
            *padded,
            pltpu.VMEM((TY, TZ, C, XL), bf16),
            pltpu.VMEM((TY, TZ, C, XL), f32),
            pltpu.VMEM((TY, TZ, C, XL), f32),
            pltpu.VMEM((TY, C * TZ, XL), f32),
            pltpu.VMEM((TY, C * TZ, XL), f32),
            pltpu.VMEM((2, NF, C, 384), bf16),
            pltpu.VMEM((C3, K9), bf16),
            pltpu.VMEM((C3, K9), bf16),
            pltpu.VMEM((C3, K9), bf16),
            pltpu.VMEM((K9, C3), f32),
            pltpu.VMEM((16, NF * 8, 128), bf16),
            pltpu.VMEM((16, NF * 8, 128), bf16),
            pltpu.VMEM((PLANE, NF * 8, 128), bf16),
            pltpu.VMEM((NF, NF * 8, 128), bf16),
            pltpu.VMEM((NF, 8, 128), f32),
            pltpu.VMEM((16, 128), bf16),
            pltpu.VMEM((PLANE, 16, 128), bf16),
            dma((2, 8)), dma((2, 8)),
            dma((2, 3)), dma((2, 3)),
            dma((2,)), dma,
            dma((3,)), dma((3,)),
            dma, dma,
        ],
        compiler_params=pltpu.CompilerParams(
            collective_id=0, has_side_effects=True, vmem_limit_bytes=60 << 20
        ),
    )(
        coarse_field[0], fine_target[0], kernel_one, kernel_two,
        moment_one, moment_two, second_one, second_two,
    )
    prediction, update_one, update_two = pl.pallas_call(
        hand_on,
        out_shape=results,
        in_specs=[vmem] * 3,
        out_specs=[hbm] * 3,
        scratch_shapes=[dma((3,))],
        compiler_params=pltpu.CompilerParams(vmem_limit_bytes=4 << 20),
    )(*computed)
    return prediction[None], update_one, update_two


def solution(mesh):
    field = P("fsdp", None, "gy", "gz", None)
    state = P(None, "fsdp")
    return jax.shard_map(
        shards,
        mesh=mesh,
        in_specs=(field, field) + (state,) * 6,
        out_specs=(field, state, state),
        check_vma=False,
    )
```
